512 devices in a mesh: rows: 32 (over x, z), cols: 16 (over y, core).
Axes of the slice: x: 4, y: 8, z: 8, core: 2. Of those that a mesh axis runs over, the one named last changes fastest.
Arguments:
- features: bfloat16 [512, 256, 256], P('rows', 'cols'), may hold values from -6 to 6
- conv_weight: bfloat16 [4, 4, 256, 256], replicated, may hold values from -0.1875 to 0.1875
- query_weight: bfloat16 [256, 256], replicated, may hold values from -0.375 to 0.375
- kv_weight: bfloat16 [256, 512], replicated, may hold values from -0.375 to 0.375
- out_weight: bfloat16 [256, 256], replicated, may hold values from -0.375 to 0.375
- queries: float32 [100, 256], replicated, may hold values from -150 to 150
- norm_gain: float32 [256], replicated, may hold values from 0.5 to 1.5
- active_blocks: int32 [100, 32], replicated, may hold values from 0 to 511, all different within a row
Outputs:
- pixels: bfloat16 [1024, 512, 256], P('rows', 'cols')
- attended: float32 [100, 256], replicated
- updated: float32 [100, 256], replicated
The draws below stay inside these ranges and needn't reach their ends.
Inputs may be any that keep to these rules, and one draw needn't show every extreme that they name: `active_blocks`: each query names 32 different blocks of 32 x 32 pixels; every block is named by some query.
All inputs are finite; a program needn't handle non-finite values.
Results may differ from the reference program's by a relative error of at most 0.0045.
The reference program's roundings to bfloat16 on the way count: a program that leaves them out, or rounds other values in their place, can miss the bound.
Values may be sent and summed in bfloat16 or wider, within the bound.
No kernel may reach another device: no remote copies, remote signals or barrier semaphores. Data moves between devices by JAX's collectives and lax.ppermute only.
A program may use at most 128 MiB of HBM per device.

```python
import jax
import jax.numpy as jnp
from jax import lax

C = 256
QUERIES = 100
HEADS = 8
HEAD = 32
BLOCK = 32
NR = 1024
NC = 512
NBLOCKS = 512
LIST = 32


def draw_queries(key, part):
    key = jax.random.fold_in(key, 11)
    normal_draw = jax.random.normal(jax.random.fold_in(key, 1), (QUERIES, C), jnp.float32)
    return jnp.clip(normal_draw * 3.0, -15.0, 15.0)


def levels(key, shape, pieces, low, largest):
    loudness = 1.0
    for axis_at, shards_of in pieces:
        draws = jax.random.uniform(jax.random.fold_in(jax.random.fold_in(key, 6), axis_at), (shards_of,), jnp.float32, low / len(pieces), largest / len(pieces))
        loudness = loudness * jnp.repeat(jnp.exp(draws), shape[axis_at] // shards_of).reshape((-1,) + (1,) * (len(shape) - 1 - axis_at))
    return loudness


def choose_distinct(key, rows, count, top, lift):
    sequence = jax.random.permutation(jax.random.fold_in(key, 1), count)
    pull = sequence
    for power in range(3):
        pull = pull * pull // count
    pull = pull * lift // count
    chance = jax.random.randint(jax.random.fold_in(key, 2), (rows, count), 0, 4096) + pull
    sure = jax.random.permutation(jax.random.fold_in(key, 3), rows)[jnp.arange(count) % rows]
    chance = jnp.where(jnp.arange(rows)[:, None] == sure[None, :], 1 << 14, chance)
    score = chance * count + jnp.arange(count)
    return lax.top_k(score.astype(jnp.int32), top)[1].astype(jnp.int32)


def normal_values(stream_key, extent, deviation, most, shards=(), held_as=jnp.bfloat16):
    values = deviation * jax.random.normal(stream_key, extent, jnp.float32)
    if shards:
        values = values * levels(stream_key, extent, shards, -0.22, 0.18)
    return jnp.clip(values, -most, most).astype(held_as)


def setup_inputs(seed: int = 0) -> dict:
    streams_of = jax.random.split(jax.random.key(seed), 9)
    features = normal_values(streams_of[0], (NR // 2, NC // 2, C), 1.0, 6.0, ((0, 32), (1, 16)))
    conv_weight = normal_values(streams_of[1], (4, 4, C, C), (4 * C) ** -0.5, 0.1875)
    query_weight = normal_values(streams_of[2], (C, C), C ** -0.5, 0.375)
    kv_weight = normal_values(streams_of[3], (C, 2 * C), C ** -0.5, 0.375)
    out_weight = normal_values(streams_of[4], (C, C), C ** -0.5, 0.375)
    queries = draw_queries(jax.random.fold_in(streams_of[8], 71), 0)
    norm_gain = jnp.clip(1.0 + 0.1 * jax.random.normal(streams_of[6], (C,), jnp.float32), 0.5, 1.5)
    active_blocks = choose_distinct(streams_of[7], QUERIES, NBLOCKS, LIST, 1024)
    return dict(features=features, conv_weight=conv_weight, query_weight=query_weight, kv_weight=kv_weight, out_weight=out_weight, queries=queries, norm_gain=norm_gain, active_blocks=active_blocks)


masked_low = -1e+30
tap_table = (((1, 1), (0, 3)), ((1, 2), (2, 0)))

def upsample(padded, conv_weight):
    height = padded.shape[0] - 2
    breadth = padded.shape[1] - 2
    channels = padded.shape[2]
    row_parts = []
    for row_parity in range(2):
        col_parts = []
        for col_parity in range(2):
            summed = jnp.zeros((height * breadth, conv_weight.shape[3]), jnp.float32)
            for row_offset, row_kernel in tap_table[row_parity]:
                for col_offset, col_kernel in tap_table[col_parity]:
                    window = padded[row_offset:row_offset + height, col_offset:col_offset + breadth]
                    window = window.reshape(height * breadth, channels)
                    summed = summed + jnp.dot(window, conv_weight[row_kernel, col_kernel], preferred_element_type=jnp.float32)
            col_parts.append(summed.reshape(height, breadth, -1))
        row_parts.append(jnp.stack(col_parts, axis=2))
    joined = jnp.stack(row_parts, axis=1)
    return joined.reshape(2 * height, 2 * breadth, -1).astype(jnp.bfloat16)

def project_queries(queries, query_weight):
    projected = jnp.dot(queries.astype(jnp.bfloat16), query_weight, preferred_element_type=jnp.float32) * HEAD ** (-0.5)
    return projected.astype(jnp.bfloat16).reshape(QUERIES, HEADS, HEAD)

def reference(features, conv_weight, query_weight, kv_weight, out_weight, queries, norm_gain, active_blocks):
    padded = jnp.pad(features, ((1, 1), (1, 1), (0, 0)))
    pixels = upsample(padded, conv_weight)
    projected = project_queries(queries, query_weight).astype(jnp.float32)
    blocks_across = NC // BLOCK
    block_ids = jnp.arange(NBLOCKS, dtype=jnp.int32)
    allowed = jnp.any(active_blocks[:, :, None] == block_ids[None, None, :], axis=1)
    column_block = jnp.arange(NC, dtype=jnp.int32) // BLOCK

    def slab_step(running, slab_index):
        highest, totals, summed = running
        start = (slab_index * BLOCK).astype(jnp.int32)
        slab = lax.dynamic_slice_in_dim(pixels, start, BLOCK, 0).reshape(BLOCK * NC, C)
        key_value = jnp.dot(slab, kv_weight, preferred_element_type=jnp.float32).astype(jnp.bfloat16)
        key_rows = key_value[:, :C].reshape(-1, HEADS, HEAD).astype(jnp.float32)
        value_rows = key_value[:, C:].reshape(-1, HEADS, HEAD).astype(jnp.float32)
        scores = jnp.einsum('qhd,phd->qhp', projected, key_rows)
        col_start = (slab_index * blocks_across).astype(jnp.int32)
        slab_allowed = lax.dynamic_slice_in_dim(allowed, col_start, blocks_across, 1)
        active = jnp.tile(slab_allowed[:, column_block], (1, BLOCK))[:, None, :]
        local_max = lax.optimization_barrier(jnp.max(jnp.where(active, scores, masked_low), axis=2))
        weights = jnp.where(active, jnp.exp(scores - local_max[:, :, None]), 0.0)
        weights = lax.optimization_barrier(weights.astype(jnp.bfloat16)).astype(jnp.float32)
        block_total = lax.optimization_barrier(jnp.sum(weights, axis=2))
        block_sum = jnp.einsum('qhp,phd->qhd', weights, value_rows)
        merged = jnp.maximum(highest, local_max)
        old_factor = jnp.exp(highest - merged)
        new_factor = jnp.exp(local_max - merged)
        totals = totals * old_factor + block_total * new_factor
        summed = summed * old_factor[:, :, None] + block_sum * new_factor[:, :, None]
        return ((merged, totals, summed), None)
    initial = (jnp.full((QUERIES, HEADS), masked_low, jnp.float32), jnp.zeros((QUERIES, HEADS), jnp.float32), jnp.zeros((QUERIES, HEADS, HEAD), jnp.float32))
    running, _ = lax.scan(slab_step, initial, jnp.arange(NR // BLOCK, dtype=jnp.int32))
    highest, totals, summed = running
    attention = (summed / totals[:, :, None]).reshape(QUERIES, C).astype(jnp.bfloat16)
    attended = jnp.dot(attention, out_weight, preferred_element_type=jnp.float32)
    residual_sum = queries + attended
    average = lax.optimization_barrier(jnp.mean(residual_sum, axis=1, keepdims=True))
    centred = residual_sum - average
    spread = lax.optimization_barrier(jnp.mean(centred * centred, axis=1, keepdims=True))
    updated = centred * lax.rsqrt(spread + 1e-05) * norm_gain
    return (pixels, attended, updated)
```

```python
import functools

import jax
import jax.numpy as jnp
from jax import lax
from jax.experimental import pallas as pl
from jax.experimental.pallas import tpu as pltpu
from jax.sharding import PartitionSpec as P

QUERIES = 100
PADDED = 104
HEADS = 8
HEAD = 32
BLOCK = 32
C = 256
LANES = 128
ROWS_IN = 16
COLS_IN = 16
LIST = 32
PAYLOAD = C + LANES

masked_low = -1e30
tap_table = (((1, 1), (0, 3)), ((1, 2), (2, 0)))
query_chunks = ((0, 40), (40, 32), (72, 32))


def dot(a, b):
    return jnp.dot(a, b, preferred_element_type=jnp.float32)


def dot_exact(a, b):
    return jnp.dot(a, b, preferred_element_type=jnp.float32, precision=lax.Precision.HIGHEST)


def iota(shape, dim):
    return lax.broadcasted_iota(jnp.int32, shape, dim)


def local_kernel(
    x_ref, top_ref, bottom_ref, left_ref, right_ref, weight_ref, query_weight_ref, kv_weight_ref,
    queries_ref, active_blocks_ref, pixels_ref, part_ref, shifted, joined, wide_queries, keys, values, flags, spread
):
    height = ROWS_IN + 2
    middle = jnp.concatenate([top_ref[...], x_ref[...], bottom_ref[...]], axis=0)
    shifted[1] = middle.reshape(height * COLS_IN, C)
    middle = middle.astype(jnp.float32)
    column = iota((height, COLS_IN, C), 1)
    left = left_ref[...].astype(jnp.float32)
    right = right_ref[...].astype(jnp.float32)
    before = jnp.where(column == 0, left, pltpu.roll(middle, 1, 1))
    after = jnp.where(column == COLS_IN - 1, right, pltpu.roll(middle, COLS_IN - 1, 1))
    shifted[0] = before.astype(jnp.bfloat16).reshape(height * COLS_IN, C)
    shifted[2] = after.astype(jnp.bfloat16).reshape(height * COLS_IN, C)

    area = ROWS_IN * COLS_IN
    for a in range(2):
        for b in range(2):
            total = None
            for row_offset, row_kernel in tap_table[a]:
                for col_offset, col_kernel in tap_table[b]:
                    window = shifted[col_offset, row_offset * COLS_IN : row_offset * COLS_IN + area]
                    term = dot(window, weight_ref[row_kernel, col_kernel])
                    total = term if total is None else total + term
            for half in range(2):
                part = total[:, half * LANES : (half + 1) * LANES].reshape(ROWS_IN, COLS_IN, LANES)
                joined[half, :, a, pl.ds(b, COLS_IN, stride=2), :] = part
            key_value = dot(total.astype(jnp.bfloat16), kv_weight_ref[...]).astype(jnp.bfloat16)
            at = (2 * a + b) * area
            keys[at : at + area] = key_value[:, :C]
            values[at : at + area] = key_value[:, C:]
    for half in range(2):
        part = joined[half].reshape(2 * ROWS_IN, 2 * COLS_IN, LANES).astype(jnp.bfloat16)
        pixels_ref[:, :, half * LANES : (half + 1) * LANES] = part

    projected = dot(queries_ref[...].astype(jnp.bfloat16), query_weight_ref[...]) * HEAD ** (-0.5)
    spread[:QUERIES] = projected
    spread[QUERIES:] = jnp.zeros((PADDED - QUERIES, C), jnp.float32)
    own_head = iota((1, HEADS, C), 2) // HEAD == iota((1, HEADS, C), 1)
    each = jnp.where(own_head, spread[...][:, None, :], 0.0)
    wide_queries[...] = each.reshape(PADDED * HEADS, C).astype(jnp.bfloat16)

    block_id = lax.axis_index("rows") * lax.axis_size("cols") + lax.axis_index("cols")
    hits = (active_blocks_ref[...] == block_id).astype(jnp.float32)
    flags[:QUERIES] = jnp.broadcast_to(jnp.max(hits, axis=1, keepdims=True), (QUERIES, LANES))
    flags[QUERIES:] = jnp.zeros((PADDED - QUERIES, LANES), jnp.float32)
    lane = iota((1, HEADS, LANES), 2)
    head = iota((1, HEADS, LANES), 1)
    ones = jnp.ones((4 * area, LANES), jnp.bfloat16)
    for start, count in query_chunks:
        rows = slice(start * HEADS, (start + count) * HEADS)
        now = lax.dot_general(
            wide_queries[rows], keys[...], (((1,), (1,)), ((), ())), preferred_element_type=jnp.float32
        )
        highest = jnp.max(now, axis=1, keepdims=True)
        weights = jnp.exp(now - highest).astype(jnp.bfloat16)
        summed = dot(weights, values[...]).reshape(count, HEADS, C)
        totals = dot(weights, ones).reshape(count, HEADS, LANES)
        highest = jnp.broadcast_to(highest, (count * HEADS, LANES)).reshape(count, HEADS, LANES)
        here = flags[start : start + count] > 0.0
        summed = jnp.sum(jnp.where(own_head, summed, 0.0), axis=1)
        part_ref[start : start + count, :C] = jnp.where(here[:, :1], summed, 0.0)
        totals = jnp.sum(jnp.where(lane == head + HEADS, totals, 0.0), axis=1)
        highest = jnp.sum(jnp.where(lane == head, highest, 0.0), axis=1)
        low = jnp.where(iota((count, LANES), 1) < HEADS, masked_low, 0.0)
        part_ref[start : start + count, C:] = jnp.where(here, totals + highest, low)


def local(x, top, bottom, left, right, weight, query_weight, kv_weight, queries, active_blocks):
    area = ROWS_IN * COLS_IN
    return pl.pallas_call(
        local_kernel,
        out_shape=(
            jax.ShapeDtypeStruct((2 * ROWS_IN, 2 * COLS_IN, C), jnp.bfloat16),
            jax.ShapeDtypeStruct((PADDED, PAYLOAD), jnp.float32),
        ),
        in_specs=[pl.BlockSpec(memory_space=pltpu.VMEM)] * 10,
        out_specs=[pl.BlockSpec(memory_space=pltpu.VMEM)] * 2,
        scratch_shapes=[
            pltpu.VMEM((3, (ROWS_IN + 2) * COLS_IN, C), jnp.bfloat16),
            pltpu.VMEM((2, ROWS_IN, 2, 2 * COLS_IN, LANES), jnp.float32),
            pltpu.VMEM((PADDED * HEADS, C), jnp.bfloat16),
            pltpu.VMEM((4 * area, C), jnp.bfloat16),
            pltpu.VMEM((4 * area, C), jnp.bfloat16),
            pltpu.VMEM((PADDED, LANES), jnp.float32),
            pltpu.VMEM((PADDED, C), jnp.float32),
        ],
        compiler_params=pltpu.CompilerParams(vmem_limit_bytes=40 << 20),
        cost_estimate=pl.CostEstimate(flops=2_000_000_000, bytes_accessed=4_000_000, transcendentals=800_000),
    )(x, top, bottom, left, right, weight, query_weight, kv_weight, queries, active_blocks)


def widening():
    return (iota((LANES, C), 1) // HEAD == iota((LANES, C), 0)).astype(jnp.float32)


def merge(parts):
    n, q, _ = parts.shape
    side = parts[:, :, C:]
    top = jnp.max(side, axis=0)
    is_max = iota((n, q, LANES), 2) < HEADS
    factor = jnp.where(is_max, jnp.exp(jnp.where(is_max, side - top[None], 0.0)), 0.0)
    wide = dot_exact(factor.reshape(n * q, LANES), widening()).reshape(n, q, C)
    summed = jnp.sum(parts[:, :, :C] * wide, axis=0)
    moved = pltpu.roll(factor.reshape(n * q, LANES), HEADS, 1).reshape(n, q, LANES)
    totals = jnp.sum(side * moved, axis=0)
    return summed, jnp.where(iota((q, LANES), 1) < HEADS, top, totals)


def merge_kernel(parts_ref, out_ref):
    summed, side = merge(parts_ref[...])
    out_ref[:, :, :C] = jnp.broadcast_to(summed[None], (out_ref.shape[0], *summed.shape))
    out_ref[:, :, C:] = jnp.broadcast_to(side[None], (out_ref.shape[0], *side.shape))


def attend_kernel(parts_ref, out_ref):
    summed, side = merge(parts_ref[...])
    q = side.shape[0]
    totals = pltpu.roll(side, LANES - HEADS, 1)
    totals = jnp.where(iota((q, LANES), 1) < HEADS, totals, 0.0)
    out_ref[...] = summed / dot_exact(totals, widening())


def finish_kernel(attention_ref, out_weight_ref, queries_ref, gain_ref, attended_ref, updated_ref):
    attention = attention_ref[...].reshape(-1, C)[:PADDED].astype(jnp.bfloat16)
    attended = dot(attention, out_weight_ref[...])[:QUERIES]
    attended_ref[...] = attended
    residual_sum = queries_ref[...] + attended
    average = jnp.mean(residual_sum, axis=1, keepdims=True)
    centred = residual_sum - average
    deviation = jnp.mean(centred * centred, axis=1, keepdims=True)
    updated_ref[...] = centred * lax.rsqrt(deviation + 1e-05) * gain_ref[...]


def on_device(kernel, out_shape, *operands):
    return pl.pallas_call(
        kernel,
        out_shape=out_shape,
        in_specs=[pl.BlockSpec(memory_space=pltpu.VMEM)] * len(operands),
        out_specs=jax.tree.map(lambda _: pl.BlockSpec(memory_space=pltpu.VMEM), out_shape),
        compiler_params=pltpu.CompilerParams(vmem_limit_bytes=32 << 20),
        cost_estimate=pl.CostEstimate(flops=10_000_000, bytes_accessed=500_000, transcendentals=10_000),
    )(*operands)


def neighbours(x, axis, dim):
    peers = lax.axis_size(axis)
    up = [(i, i + 1) for i in range(peers - 1)]
    down = [(j, i) for i, j in up]
    last = lax.slice_in_dim(x, x.shape[dim] - 1, x.shape[dim], axis=dim)
    first = lax.slice_in_dim(x, 0, 1, axis=dim)
    return lax.ppermute(last, axis, up), lax.ppermute(first, axis, down)


def body(
    features, conv_weight, query_weight, kv_weight, out_weight, queries, norm_gain, active_blocks
):
    top, bottom = neighbours(features, "rows", 0)
    edges = jnp.concatenate(
        [jnp.concatenate([part[:, :1], part[:, -1:]], axis=1) for part in (top, features, bottom)], axis=0
    )
    left, right = neighbours(edges, "cols", 1)
    pixels, part = local(
        features, top, bottom, left, right, conv_weight, query_weight, kv_weight, queries, active_blocks
    )
    peers = lax.axis_size("cols")
    share = 8
    part = jnp.pad(part, ((0, peers * share - PADDED), (0, 0))).reshape(peers, share, PAYLOAD)
    parts = lax.all_to_all(part, "cols", 0, 0)
    copies = jax.ShapeDtypeStruct((lax.axis_size("rows"), share, PAYLOAD), jnp.float32)
    parts = lax.all_to_all(on_device(merge_kernel, copies, parts), "rows", 0, 0)
    attention = on_device(attend_kernel, jax.ShapeDtypeStruct((share, C), jnp.float32), parts)
    attention = lax.all_gather(attention, "cols")
    out = jax.ShapeDtypeStruct((QUERIES, C), jnp.float32)
    attended, updated = on_device(
        finish_kernel, (out, out), attention, out_weight, queries, norm_gain.reshape(1, C)
    )
    return (pixels, attended, updated)


def solution(mesh):
    placed = (P("rows", "cols", None), P(), P(), P(), P(), P(), P(), P())
    return jax.shard_map(
        body,
        mesh=mesh,
        in_specs=placed,
        out_specs=(P("rows", "cols", None), P(), P()),
        check_vma=False,
    )
```

```python
import functools

import jax
import jax.numpy as jnp
from jax import lax
from jax.experimental import pallas as pl
from jax.experimental.pallas import tpu as pltpu
from jax.sharding import PartitionSpec as P

QUERIES = 100
PADDED = 104
HEADS = 8
HEAD = 32
BLOCK = 32
C = 256
LANES = 128
ROWS_IN = 16
COLS_IN = 16
LIST = 32
PAYLOAD = C + LANES

masked_low = -1e30
tap_table = (((1, 1), (0, 3)), ((1, 2), (2, 0)))
query_chunks = ((0, 40), (40, 32), (72, 32))


def dot(a, b):
    return jnp.dot(a, b, preferred_element_type=jnp.float32)


def dot_exact(a, b):
    return jnp.dot(a, b, preferred_element_type=jnp.float32, precision=lax.Precision.HIGHEST)


def iota(shape, dim):
    return lax.broadcasted_iota(jnp.int32, shape, dim)


def local_kernel(
    x_hbm, top_ref, bottom_ref, left_ref, right_ref, weight_hbm, query_weight_hbm, kv_weight_hbm,
    queries_hbm, named_hbm, pixels_hbm, part_ref,
    x_ref, weight_ref, query_weight_ref, kv_weight_ref, queries_ref, named_ref, pixels_ref,
    shifted, joined, wide_queries, keys, values, flags, spread, arrived, sent
):
    def fetch(source, target, slot):
        copy = pltpu.make_async_copy(source, target, arrived.at[slot])
        copy.start()
        return copy

    fetch_queries = fetch(queries_hbm, queries_ref, 0)
    fetch_query_weight = fetch(query_weight_hbm, query_weight_ref, 1)
    fetch_named = fetch(named_hbm, named_ref, 2)
    fetch_x = fetch(x_hbm, x_ref, 3)
    fetch_weight = {}
    for a in range(2):
        for _, row_kernel in tap_table[a]:
            fetch_weight[row_kernel] = fetch(
                weight_hbm.at[row_kernel], weight_ref.at[row_kernel], 4 + row_kernel
            )
        if a == 0:
            fetch_kv_weight = fetch(kv_weight_hbm, kv_weight_ref, 8)

    own_head = iota((1, HEADS, C), 2) // HEAD == iota((1, HEADS, C), 1)
    fetch_queries.wait()
    fetch_query_weight.wait()
    projected = dot(queries_ref[...].astype(jnp.bfloat16), query_weight_ref[...]) * HEAD ** (-0.5)
    spread[:QUERIES] = projected
    spread[QUERIES:] = jnp.zeros((PADDED - QUERIES, C), jnp.float32)
    each = jnp.where(own_head, spread[...][:, None, :], 0.0)
    wide_queries[...] = each.reshape(PADDED * HEADS, C).astype(jnp.bfloat16)

    fetch_named.wait()
    block_id = lax.axis_index("rows") * lax.axis_size("cols") + lax.axis_index("cols")
    hits = (named_ref[...] == block_id).astype(jnp.bfloat16)
    flags[:QUERIES] = lax.dot_general(
        hits, jnp.ones((hits.shape[0], LANES), jnp.bfloat16), (((0,), (0,)), ((), ())), preferred_element_type=jnp.float32
    )
    flags[QUERIES:] = jnp.zeros((PADDED - QUERIES, LANES), jnp.float32)

    fetch_x.wait()
    height = ROWS_IN + 2
    middle = jnp.concatenate([top_ref[...], x_ref[...], bottom_ref[...]], axis=0)
    shifted[1] = middle.reshape(height * COLS_IN, C)
    middle = middle.astype(jnp.float32)
    column = iota((height, COLS_IN, C), 1)
    left = left_ref[...].astype(jnp.float32)
    right = right_ref[...].astype(jnp.float32)
    before = jnp.where(column == 0, left, pltpu.roll(middle, 1, 1))
    after = jnp.where(column == COLS_IN - 1, right, pltpu.roll(middle, COLS_IN - 1, 1))
    shifted[0] = before.astype(jnp.bfloat16).reshape(height * COLS_IN, C)
    shifted[2] = after.astype(jnp.bfloat16).reshape(height * COLS_IN, C)

    area = ROWS_IN * COLS_IN
    for a in range(2):
        for _, row_kernel in tap_table[a]:
            fetch_weight[row_kernel].wait()
        if a == 0:
            fetch_kv_weight.wait()
        for b in range(2):
            total = None
            for row_offset, row_kernel in tap_table[a]:
                for col_offset, col_kernel in tap_table[b]:
                    window = shifted[col_offset, row_offset * COLS_IN : row_offset * COLS_IN + area]
                    term = dot(window, weight_ref[row_kernel, col_kernel])
                    total = term if total is None else total + term
            for half in range(2):
                part = total[:, half * LANES : (half + 1) * LANES].reshape(ROWS_IN, COLS_IN, LANES)
                joined[half, :, a, pl.ds(b, COLS_IN, stride=2), :] = part
            key_value = dot(total.astype(jnp.bfloat16), kv_weight_ref[...]).astype(jnp.bfloat16)
            at = (2 * a + b) * area
            keys[at : at + area] = key_value[:, :C]
            values[at : at + area] = key_value[:, C:]
    for half in range(2):
        part = joined[half].reshape(2 * ROWS_IN, 2 * COLS_IN, LANES).astype(jnp.bfloat16)
        pixels_ref[:, :, half * LANES : (half + 1) * LANES] = part
    send_pixels = pltpu.make_async_copy(pixels_ref, pixels_hbm, sent)
    send_pixels.start()

    lane = iota((1, HEADS, LANES), 2)
    head = iota((1, HEADS, LANES), 1)
    ones = jnp.ones((4 * area, LANES), jnp.bfloat16)
    for start, count in query_chunks:
        rows = slice(start * HEADS, (start + count) * HEADS)
        now = lax.dot_general(
            wide_queries[rows], keys[...], (((1,), (1,)), ((), ())), preferred_element_type=jnp.float32
        )
        highest = jnp.max(now, axis=1, keepdims=True)
        weights = jnp.exp(now - highest).astype(jnp.bfloat16)
        summed = dot(weights, values[...]).reshape(count, HEADS, C)
        totals = dot(weights, ones).reshape(count, HEADS, LANES)
        highest = jnp.broadcast_to(highest, (count * HEADS, LANES)).reshape(count, HEADS, LANES)
        here = flags[start : start + count] > 0.0
        summed = jnp.sum(jnp.where(own_head, summed, 0.0), axis=1)
        share = part_ref.shape[1]
        shares = slice(start // share, (start + count) // share)
        part_ref[shares, :, :C] = jnp.where(here[:, :1], summed, 0.0).reshape(-1, share, C)
        totals = jnp.sum(jnp.where(lane == head + HEADS, totals, 0.0), axis=1)
        highest = jnp.sum(jnp.where(lane == head, highest, 0.0), axis=1)
        low = jnp.where(iota((count, LANES), 1) < HEADS, masked_low, 0.0)
        part_ref[shares, :, C:] = jnp.where(here, totals + highest, low).reshape(-1, share, LANES)
    filled = PADDED // share
    if filled < part_ref.shape[0]:
        part_ref[filled:] = jnp.zeros((part_ref.shape[0] - filled, share, PAYLOAD), jnp.float32)
    send_pixels.wait()


def local(x, top, bottom, left, right, weight, query_weight, kv_weight, queries, active_blocks, part_shape):
    area = ROWS_IN * COLS_IN
    pixels = jax.ShapeDtypeStruct((2 * ROWS_IN, 2 * COLS_IN, C), jnp.bfloat16)
    vmem = pl.BlockSpec(memory_space=pltpu.VMEM)
    hbm = pl.BlockSpec(memory_space=pltpu.HBM)
    named = active_blocks.T
    return pl.pallas_call(
        local_kernel,
        out_shape=(pixels, jax.ShapeDtypeStruct(part_shape, jnp.float32)),
        in_specs=[hbm] + [vmem] * 4 + [hbm] * 5,
        out_specs=[hbm, vmem],
        scratch_shapes=[pltpu.VMEM(t.shape, t.dtype) for t in (x, weight, query_weight, kv_weight, queries, named, pixels)]
        + [
            pltpu.VMEM((3, (ROWS_IN + 2) * COLS_IN, C), jnp.bfloat16),
            pltpu.VMEM((2, ROWS_IN, 2, 2 * COLS_IN, LANES), jnp.float32),
            pltpu.VMEM((PADDED * HEADS, C), jnp.bfloat16),
            pltpu.VMEM((4 * area, C), jnp.bfloat16),
            pltpu.VMEM((4 * area, C), jnp.bfloat16),
            pltpu.VMEM((PADDED, LANES), jnp.float32),
            pltpu.VMEM((PADDED, C), jnp.float32),
            pltpu.SemaphoreType.DMA((9,)),
            pltpu.SemaphoreType.DMA,
        ],
        compiler_params=pltpu.CompilerParams(vmem_limit_bytes=60 << 20),
        cost_estimate=pl.CostEstimate(flops=2_000_000_000, bytes_accessed=4_000_000, transcendentals=800_000),
    )(x, top, bottom, left, right, weight, query_weight, kv_weight, queries, named)


def widening():
    return (iota((LANES, C), 1) // HEAD == iota((LANES, C), 0)).astype(jnp.float32)


def merge(parts):
    n, q, _ = parts.shape
    side = parts[:, :, C:]
    top = jnp.max(side, axis=0)
    is_max = iota((n, q, LANES), 2) < HEADS
    factor = jnp.where(is_max, jnp.exp(jnp.where(is_max, side - top[None], 0.0)), 0.0)
    wide = dot_exact(factor.reshape(n * q, LANES), widening()).reshape(n, q, C)
    summed = jnp.sum(parts[:, :, :C] * wide, axis=0)
    moved = pltpu.roll(factor.reshape(n * q, LANES), HEADS, 1).reshape(n, q, LANES)
    totals = jnp.sum(side * moved, axis=0)
    return summed, jnp.where(iota((q, LANES), 1) < HEADS, top, totals)


def copied(x, shape):
    return jnp.broadcast_to(x[None], shape).astype(jnp.float32)


def merge_kernel(parts_ref, out_ref):
    summed, side = merge(parts_ref[...])
    out_ref[:, :, :C] = copied(summed, (out_ref.shape[0], *summed.shape))
    out_ref[:, :, C:] = copied(side, (out_ref.shape[0], *side.shape))


def attend_kernel(parts_ref, out_ref):
    summed, side = merge(parts_ref[...])
    q = side.shape[0]
    totals = pltpu.roll(side, LANES - HEADS, 1)
    totals = jnp.where(iota((q, LANES), 1) < HEADS, totals, 0.0)
    attention = summed / dot_exact(totals, widening())
    out_ref[...] = copied(attention, out_ref.shape).astype(out_ref.dtype)


def finish_kernel(attention_ref, out_weight_ref, queries_ref, gain_ref, attended_ref, updated_ref):
    attention = attention_ref[...].astype(jnp.float32).reshape(-1, C)[:PADDED].astype(jnp.bfloat16)
    attended = dot(attention, out_weight_ref[...])[:QUERIES]
    attended_ref[...] = attended
    residual_sum = queries_ref[...] + attended
    average = jnp.mean(residual_sum, axis=1, keepdims=True)
    centred = residual_sum - average
    deviation = jnp.mean(centred * centred, axis=1, keepdims=True)
    updated_ref[...] = centred * lax.rsqrt(deviation + 1e-05) * gain_ref[...]


def on_device(kernel, out_shape, *operands):
    return pl.pallas_call(
        kernel,
        out_shape=out_shape,
        in_specs=[pl.BlockSpec(memory_space=pltpu.VMEM)] * len(operands),
        out_specs=jax.tree.map(lambda _: pl.BlockSpec(memory_space=pltpu.VMEM), out_shape),
        compiler_params=pltpu.CompilerParams(vmem_limit_bytes=32 << 20),
        cost_estimate=pl.CostEstimate(flops=10_000_000, bytes_accessed=500_000, transcendentals=10_000),
    )(*operands)


def neighbours(x, axis, dim):
    peers = lax.axis_size(axis)
    up = [(i, i + 1) for i in range(peers - 1)]
    down = [(j, i) for i, j in up]
    last = lax.slice_in_dim(x, x.shape[dim] - 1, x.shape[dim], axis=dim)
    first = lax.slice_in_dim(x, 0, 1, axis=dim)
    return lax.ppermute(last, axis, up), lax.ppermute(first, axis, down)


def body(
    features, conv_weight, query_weight, kv_weight, out_weight, queries, norm_gain, active_blocks
):
    top, bottom = neighbours(features, "rows", 0)
    edges = jnp.concatenate(
        [jnp.concatenate([part[:, :1], part[:, -1:]], axis=1) for part in (top, features, bottom)], axis=0
    )
    left, right = neighbours(edges, "cols", 1)
    row_peers, col_peers = lax.axis_size("rows"), lax.axis_size("cols")
    share = pl.cdiv(QUERIES, row_peers)
    pixels, part = local(
        features, top, bottom, left, right, conv_weight, query_weight, kv_weight, queries, active_blocks,
        (row_peers, share, PAYLOAD),
    )
    parts = lax.all_to_all(part, "rows", 0, 0)
    copies = jax.ShapeDtypeStruct((col_peers, share, PAYLOAD), jnp.float32)
    parts = lax.all_to_all(on_device(merge_kernel, copies, parts), "cols", 0, 0)
    copies = jax.ShapeDtypeStruct((row_peers, share, C), jnp.bfloat16)
    attention = lax.all_to_all(on_device(attend_kernel, copies, parts), "rows", 0, 0)
    out = jax.ShapeDtypeStruct((QUERIES, C), jnp.float32)
    attended, updated = on_device(
        finish_kernel, (out, out), attention, out_weight, queries, norm_gain.reshape(1, C)
    )
    return (pixels, attended, updated)


def solution(mesh):
    placed = (P("rows", "cols", None), P(), P(), P(), P(), P(), P(), P())
    return jax.shard_map(
        body,
        mesh=mesh,
        in_specs=placed,
        out_specs=(P("rows", "cols", None), P(), P()),
        check_vma=False,
    )
```

```python
import functools

import jax
import jax.numpy as jnp
from jax import lax
from jax.experimental import pallas as pl
from jax.experimental.pallas import tpu as pltpu
from jax.sharding import PartitionSpec as P

QUERIES = 100
PADDED = 104
HEADS = 8
HEAD = 32
BLOCK = 32
C = 256
LANES = 128
ROWS_IN = 16
COLS_IN = 16
LIST = 32
HALF = HEADS // 2
SHARE = 7
TILE = 8
HALVES = 2 * PADDED

masked_low = -1e30
tap_table = (((1, 1), (0, 3)), ((1, 2), (2, 0)))
query_chunks = ((0, 40), (40, 32), (72, 32))


def dot(a, b):
    return jnp.dot(a, b, preferred_element_type=jnp.float32)


def dot_exact(a, b):
    return jnp.dot(a, b, preferred_element_type=jnp.float32, precision=lax.Precision.HIGHEST)


def iota(shape, dim):
    return lax.broadcasted_iota(jnp.int32, shape, dim)


def local_kernel(
    x_hbm, top_hbm, bottom_hbm, left_hbm, right_hbm, weight_hbm, query_weight_hbm, kv_weight_hbm,
    queries_hbm, named_hbm, pixels_hbm, part_hbm,
    padded, left_ref, right_ref, weight_ref, query_weight_ref, kv_weight_ref, queries_ref, named_ref, pixels_ref, part_ref,
    shifted, joined, wide_queries, keys, values, flags, spread, half_sums, half_side, arrived, sent
):
    def fetch(source, target, slot):
        copy = pltpu.make_async_copy(source, target, arrived.at[slot])
        copy.start()
        return copy

    fetch_queries = fetch(queries_hbm, queries_ref, 0)
    fetch_query_weight = fetch(query_weight_hbm, query_weight_ref, 1)
    fetch_named = fetch(named_hbm, named_ref, 2)
    fetch_features = [
        fetch(top_hbm, padded.at[pl.ds(0, 1)], 3),
        fetch(x_hbm, padded.at[pl.ds(1, ROWS_IN)], 9),
        fetch(bottom_hbm, padded.at[pl.ds(ROWS_IN + 1, 1)], 10),
        fetch(left_hbm, left_ref, 11),
        fetch(right_hbm, right_ref, 12),
    ]
    fetch_weight = {}
    for a in range(2):
        for _, row_kernel in tap_table[a]:
            fetch_weight[row_kernel] = fetch(
                weight_hbm.at[row_kernel], weight_ref.at[row_kernel], 4 + row_kernel
            )
        if a == 0:
            fetch_kv_weight = fetch(kv_weight_hbm, kv_weight_ref, 8)

    own_head = iota((1, HEADS, C), 2) // HEAD == iota((1, HEADS, C), 1)
    fetch_queries.wait()
    fetch_query_weight.wait()
    projected = dot(queries_ref[...].astype(jnp.bfloat16), query_weight_ref[...]) * HEAD ** (-0.5)
    spread[:QUERIES] = projected
    spread[QUERIES:] = jnp.zeros((PADDED - QUERIES, C), jnp.float32)
    each = jnp.where(own_head, spread[...][:, None, :], 0.0)
    wide_queries[...] = each.reshape(PADDED * HEADS, C).astype(jnp.bfloat16)

    fetch_named.wait()
    block_id = lax.axis_index("rows") * lax.axis_size("cols") + lax.axis_index("cols")
    hits = (named_ref[...] == block_id).astype(jnp.bfloat16)
    flags[:QUERIES] = lax.dot_general(
        hits, jnp.ones((hits.shape[0], LANES), jnp.bfloat16), (((0,), (0,)), ((), ())), preferred_element_type=jnp.float32
    )
    flags[QUERIES:] = jnp.zeros((PADDED - QUERIES, LANES), jnp.float32)

    for copy in fetch_features:
        copy.wait()
    height = ROWS_IN + 2
    middle = padded[...]
    shifted[1] = middle.reshape(height * COLS_IN, C)
    middle = middle.astype(jnp.float32)
    column = iota((height, COLS_IN, C), 1)
    left = left_ref[...].astype(jnp.float32)
    right = right_ref[...].astype(jnp.float32)
    before = jnp.where(column == 0, left, pltpu.roll(middle, 1, 1))
    after = jnp.where(column == COLS_IN - 1, right, pltpu.roll(middle, COLS_IN - 1, 1))
    shifted[0] = before.astype(jnp.bfloat16).reshape(height * COLS_IN, C)
    shifted[2] = after.astype(jnp.bfloat16).reshape(height * COLS_IN, C)

    area = ROWS_IN * COLS_IN
    for a in range(2):
        for _, row_kernel in tap_table[a]:
            fetch_weight[row_kernel].wait()
        if a == 0:
            fetch_kv_weight.wait()
        for b in range(2):
            total = None
            for row_offset, row_kernel in tap_table[a]:
                for col_offset, col_kernel in tap_table[b]:
                    window = shifted[col_offset, row_offset * COLS_IN : row_offset * COLS_IN + area]
                    term = dot(window, weight_ref[row_kernel, col_kernel])
                    total = term if total is None else total + term
            for half in range(2):
                part = total[:, half * LANES : (half + 1) * LANES].reshape(ROWS_IN, COLS_IN, LANES)
                joined[half, :, a, pl.ds(b, COLS_IN, stride=2), :] = part
            key_value = dot(total.astype(jnp.bfloat16), kv_weight_ref[...]).astype(jnp.bfloat16)
            at = (2 * a + b) * area
            keys[at : at + area] = key_value[:, :C]
            values[at : at + area] = key_value[:, C:]
    for half in range(2):
        part = joined[half].reshape(2 * ROWS_IN, 2 * COLS_IN, LANES).astype(jnp.bfloat16)
        pixels_ref[:, :, half * LANES : (half + 1) * LANES] = part
    send_pixels = pltpu.make_async_copy(pixels_ref, pixels_hbm, sent.at[0])
    send_pixels.start()

    ones = jnp.ones((4 * area, LANES), jnp.bfloat16)
    for start, count in query_chunks:
        rows = slice(start * HEADS, (start + count) * HEADS)
        now = lax.dot_general(
            wide_queries[rows], keys[...], (((1,), (1,)), ((), ())), preferred_element_type=jnp.float32
        )
        highest = jnp.max(now, axis=1, keepdims=True)
        weights = jnp.exp(now - highest).astype(jnp.bfloat16)
        summed = dot(weights, values[...]).reshape(count, HEADS, C)
        totals = dot(weights, ones).reshape(count, HEADS, LANES)
        highest = jnp.broadcast_to(highest, (count * HEADS, LANES)).reshape(count, HEADS, LANES)
        here = flags[start : start + count] > 0.0
        summed = jnp.sum(jnp.where(own_head, summed, 0.0), axis=1)
        lane = iota((count, HEADS, LANES), 2)
        head = iota((count, HEADS, LANES), 1)
        for half in range(2):
            at = half * PADDED + start
            into = slice(at, at + count)
            half_sums[into] = jnp.where(here, summed[:, half * LANES : (half + 1) * LANES], 0.0)
            row = lax.rem(iota((count, HEADS, LANES), 0) + at, SHARE)
            slot = lane - TILE * row
            own = head - HALF * half
            own = jnp.where((own >= 0) & (own < HALF), own, -TILE * LANES)
            is_highest = slot == own
            placed = jnp.where(is_highest, highest, 0.0) + jnp.where(slot == own + HALF, totals, 0.0)
            absent = jnp.sum(jnp.where(is_highest, masked_low, 0.0), axis=1)
            half_side[into] = jnp.where(here, jnp.sum(placed, axis=1), absent)

    for buffer in (half_sums, half_side):
        buffer[HALVES:] = jnp.zeros((buffer.shape[0] - HALVES, LANES), jnp.float32)
    filled = pl.cdiv(HALVES, SHARE)
    for index in range(filled):
        rows = slice(index * SHARE, (index + 1) * SHARE)
        part_ref[index, :SHARE] = half_sums[rows]
        part_ref[index, SHARE:] = jnp.sum(half_side[rows], axis=0, keepdims=True)
    if filled < part_ref.shape[0]:
        part_ref[filled:] = jnp.zeros((part_ref.shape[0] - filled, TILE, LANES), jnp.float32)
    send_part = pltpu.make_async_copy(part_ref, part_hbm, sent.at[1])
    send_part.start()
    send_pixels.wait()
    send_part.wait()


def local(x, top, bottom, left, right, weight, query_weight, kv_weight, queries, active_blocks, shares):
    area = ROWS_IN * COLS_IN
    pixels = jax.ShapeDtypeStruct((2 * ROWS_IN, 2 * COLS_IN, C), jnp.bfloat16)
    padded = jax.ShapeDtypeStruct((ROWS_IN + 2, COLS_IN, C), jnp.bfloat16)
    part = jax.ShapeDtypeStruct((shares, TILE, LANES), jnp.float32)
    anywhere = pl.BlockSpec(memory_space=pl.ANY)
    named = active_blocks.T
    return pl.pallas_call(
        local_kernel,
        out_shape=(pixels, part),
        in_specs=[anywhere] * 10,
        out_specs=[anywhere] * 2,
        scratch_shapes=[pltpu.VMEM(t.shape, t.dtype) for t in (padded, left, right, weight, query_weight, kv_weight, queries, named, pixels, part)]
        + [
            pltpu.VMEM((3, (ROWS_IN + 2) * COLS_IN, C), jnp.bfloat16),
            pltpu.VMEM((2, ROWS_IN, 2, 2 * COLS_IN, LANES), jnp.float32),
            pltpu.VMEM((PADDED * HEADS, C), jnp.bfloat16),
            pltpu.VMEM((4 * area, C), jnp.bfloat16),
            pltpu.VMEM((4 * area, C), jnp.bfloat16),
            pltpu.VMEM((PADDED, LANES), jnp.float32),
            pltpu.VMEM((PADDED, C), jnp.float32),
            pltpu.VMEM((HALVES + TILE, LANES), jnp.float32),
            pltpu.VMEM((HALVES + TILE, LANES), jnp.float32),
            pltpu.SemaphoreType.DMA((13,)),
            pltpu.SemaphoreType.DMA((2,)),
        ],
        compiler_params=pltpu.CompilerParams(vmem_limit_bytes=60 << 20),
        cost_estimate=pl.CostEstimate(flops=2_000_000_000, bytes_accessed=4_000_000, transcendentals=800_000),
    )(x, top, bottom, left, right, weight, query_weight, kv_weight, queries, named)


def widened(side, first):
    n = side.shape[0]
    lane = iota((n, TILE, LANES), 2)
    own = lane // TILE == iota((n, TILE, LANES), 1)
    rows = jnp.where(own, jnp.broadcast_to(side, (n, TILE, LANES)), 0.0).reshape(n * TILE, LANES)
    spread = iota((LANES, LANES), 0) % TILE - first == iota((LANES, LANES), 1) // HEAD
    return dot_exact(rows, spread.astype(jnp.float32)).reshape(n, TILE, LANES)


def merge(parts):
    n = parts.shape[0]
    side = parts[:, SHARE:, :]
    lane = iota((n, 1, LANES), 2)
    is_highest = (lane % TILE < HALF) & (lane < SHARE * TILE)
    top = jnp.max(side, axis=0, keepdims=True)
    factor = jnp.where(is_highest, jnp.exp(jnp.where(is_highest, side - top, 0.0)), 0.0)
    summed = jnp.sum(parts * widened(factor, 0), axis=0)
    moved = pltpu.roll(factor.reshape(n, LANES), HALF, 1)
    totals = jnp.sum(side.reshape(n, LANES) * moved, axis=0, keepdims=True)
    return summed, jnp.where(is_highest[0], top[0], totals)


def merge_kernel(parts_ref, out_ref):
    summed, side = merge(parts_ref[...])
    row = iota((TILE, LANES), 0)
    merged = jnp.where(row == SHARE, jnp.broadcast_to(side, (TILE, LANES)), summed)
    out_ref[...] = jnp.broadcast_to(merged[None], out_ref.shape)


def attend_kernel(parts_ref, out_ref):
    summed, side = merge(parts_ref[...])
    totals = widened(side[None], HALF)[0]
    attention = jnp.where(iota((TILE, LANES), 0) == SHARE, 0.0, summed / totals)
    out_ref[...] = jnp.broadcast_to(attention[None], out_ref.shape).astype(out_ref.dtype)


def finish_kernel(attention_ref, out_weight_ref, queries_ref, gain_ref, attended_ref, updated_ref, halves):
    shares = attention_ref[...].astype(jnp.float32)
    for index in range(pl.cdiv(HALVES, SHARE)):
        halves[index * SHARE : (index + 1) * SHARE] = shares[index, :SHARE]
    attended = jnp.zeros((PADDED, C), jnp.float32)
    for half in range(2):
        attention = halves[half * PADDED : (half + 1) * PADDED].astype(jnp.bfloat16)
        attended += dot(attention, out_weight_ref[half * LANES : (half + 1) * LANES])
    attended = attended[:QUERIES]
    attended_ref[...] = attended
    residual_sum = queries_ref[...] + attended
    average = jnp.mean(residual_sum, axis=1, keepdims=True)
    centred = residual_sum - average
    deviation = jnp.mean(centred * centred, axis=1, keepdims=True)
    updated_ref[...] = centred * lax.rsqrt(deviation + 1e-05) * gain_ref[...]


def on_device(kernel, out_shape, *operands, scratch=()):
    return pl.pallas_call(
        kernel,
        out_shape=out_shape,
        in_specs=[pl.BlockSpec(memory_space=pltpu.VMEM)] * len(operands),
        out_specs=jax.tree.map(lambda _: pl.BlockSpec(memory_space=pltpu.VMEM), out_shape),
        scratch_shapes=scratch,
        compiler_params=pltpu.CompilerParams(vmem_limit_bytes=32 << 20),
        cost_estimate=pl.CostEstimate(flops=10_000_000, bytes_accessed=500_000, transcendentals=10_000),
    )(*operands)


def neighbours(x, axis, dim):
    peers = lax.axis_size(axis)
    last = lax.slice_in_dim(x, x.shape[dim] - 1, x.shape[dim], axis=dim)
    first = lax.slice_in_dim(x, 0, 1, axis=dim)
    odd = lax.axis_index(axis) % 2 == 1
    swaps = []
    for start, edge in ((0, jnp.where(odd, first, last)), (1, jnp.where(odd, last, first))):
        pairs = [(i, i + 1) for i in range(start, peers - 1, 2)]
        swaps.append(lax.ppermute(edge, axis, pairs + [(j, i) for i, j in pairs]))
    return jnp.where(odd, swaps[0], swaps[1]), jnp.where(odd, swaps[1], swaps[0])


def body(
    features, conv_weight, query_weight, kv_weight, out_weight, queries, norm_gain, active_blocks
):
    top, bottom = neighbours(features, "rows", 0)
    edges = jnp.concatenate(
        [jnp.concatenate([part[:, :1], part[:, -1:]], axis=1) for part in (top, features, bottom)], axis=0
    )
    left, right = neighbours(edges, "cols", 1)
    row_peers, col_peers = lax.axis_size("rows"), lax.axis_size("cols")
    pixels, part = local(
        features, top, bottom, left, right, conv_weight, query_weight, kv_weight, queries, active_blocks, row_peers
    )
    parts = lax.all_to_all(part, "rows", 0, 0)
    copies = jax.ShapeDtypeStruct((col_peers, TILE, LANES), jnp.float32)
    parts = lax.all_to_all(on_device(merge_kernel, copies, parts), "cols", 0, 0)
    copies = jax.ShapeDtypeStruct((row_peers, TILE, LANES), jnp.bfloat16)
    attention = lax.all_to_all(on_device(attend_kernel, copies, parts), "rows", 0, 0)
    out = jax.ShapeDtypeStruct((QUERIES, C), jnp.float32)
    attended, updated = on_device(
        finish_kernel, (out, out), attention, out_weight, queries, norm_gain.reshape(1, C),
        scratch=[pltpu.VMEM((HALVES + TILE, LANES), jnp.float32)],
    )
    return (pixels, attended, updated)


def solution(mesh):
    placed = (P("rows", "cols", None), P(), P(), P(), P(), P(), P(), P())
    return jax.shard_map(
        body,
        mesh=mesh,
        in_specs=placed,
        out_specs=(P("rows", "cols", None), P(), P()),
        check_vma=False,
    )
```

```python
import functools

import jax
import jax.numpy as jnp
from jax import lax
from jax.experimental import pallas as pl
from jax.experimental.pallas import tpu as pltpu
from jax.sharding import PartitionSpec as P

QUERIES = 100
PADDED = 104
HEADS = 8
HEAD = 32
BLOCK = 32
C = 256
LANES = 128
ROWS_IN = 16
COLS_IN = 16
LIST = 32
HALF = HEADS // 2
SHARE = 7
TILE = 8
HALVES = 2 * PADDED

masked_low = -1e30
tap_table = (((1, 1), (0, 3)), ((1, 2), (2, 0)))


def dot(a, b):
    return jnp.dot(a, b, preferred_element_type=jnp.float32)


def dot_exact(a, b):
    return jnp.dot(a, b, preferred_element_type=jnp.float32, precision=lax.Precision.HIGHEST)


def iota(shape, dim):
    return lax.broadcasted_iota(jnp.int32, shape, dim)


def prepare_kernel(
    x_hbm, weight_hbm, query_weight_hbm, kv_weight_hbm, queries_hbm, named_hbm,
    x_ref, weight_ref, kv_weight_ref, wide_queries, flags,
    query_weight_ref, queries_ref, named_ref, spread, arrived
):
    copies = [
        pltpu.make_async_copy(source, target, arrived.at[slot])
        for slot, (source, target) in enumerate((
            (queries_hbm, queries_ref), (query_weight_hbm, query_weight_ref), (named_hbm, named_ref),
            (x_hbm, x_ref), (weight_hbm, weight_ref), (kv_weight_hbm, kv_weight_ref),
        ))
    ]
    for copy in copies:
        copy.start()

    copies[0].wait()
    copies[1].wait()
    projected = dot(queries_ref[...].astype(jnp.bfloat16), query_weight_ref[...]) * HEAD ** (-0.5)
    spread[:QUERIES] = projected
    spread[QUERIES:] = jnp.zeros((PADDED - QUERIES, C), jnp.float32)
    own_head = iota((1, HEADS, C), 2) // HEAD == iota((1, HEADS, C), 1)
    each = jnp.where(own_head, spread[...][:, None, :], 0.0)
    wide_queries[...] = each.reshape(PADDED * HEADS, C).astype(jnp.bfloat16)

    copies[2].wait()
    block_id = lax.axis_index("rows") * lax.axis_size("cols") + lax.axis_index("cols")
    hits = (named_ref[...] == block_id).astype(jnp.bfloat16)
    flags[:QUERIES] = lax.dot_general(
        hits, jnp.ones((hits.shape[0], LANES), jnp.bfloat16), (((0,), (0,)), ((), ())),
        preferred_element_type=jnp.float32,
    )
    flags[QUERIES:] = jnp.zeros((PADDED - QUERIES, LANES), jnp.float32)
    for copy in copies[3:]:
        copy.wait()


def prepare(x, weight, query_weight, kv_weight, queries, active_blocks):
    named = active_blocks.T
    operands = [
        pltpu.with_memory_space_constraint(t, pltpu.HBM)
        for t in (x, weight, query_weight, kv_weight, queries, named)
    ]
    vmem = pl.BlockSpec(memory_space=pltpu.VMEM)
    made = (
        x, weight, kv_weight,
        jax.ShapeDtypeStruct((PADDED * HEADS, C), jnp.bfloat16),
        jax.ShapeDtypeStruct((PADDED, LANES), jnp.float32),
    )
    return pl.pallas_call(
        prepare_kernel,
        out_shape=tuple(jax.ShapeDtypeStruct(t.shape, t.dtype) for t in made),
        in_specs=[pl.BlockSpec(memory_space=pltpu.HBM)] * len(operands),
        out_specs=[vmem] * len(made),
        scratch_shapes=[pltpu.VMEM(t.shape, t.dtype) for t in (query_weight, queries, named)]
        + [pltpu.VMEM((PADDED, C), jnp.float32), pltpu.SemaphoreType.DMA((6,))],
        compiler_params=pltpu.CompilerParams(vmem_limit_bytes=16 << 20),
        cost_estimate=pl.CostEstimate(flops=20_000_000, bytes_accessed=6_000_000, transcendentals=0),
    )(*operands)


def local_kernel(
    x_ref, top_ref, bottom_ref, left_ref, right_ref, weight_ref, kv_weight_ref, wide_queries, flags,
    pixels_hbm, part_ref,
    pixels_ref, shifted, joined, keys, values, half_sums, half_side, sent
):
    height = ROWS_IN + 2
    middle = jnp.concatenate([top_ref[...], x_ref[...], bottom_ref[...]], axis=0)
    shifted[1] = middle.reshape(height * COLS_IN, C)
    middle = middle.astype(jnp.float32)
    column = iota((height, COLS_IN, C), 1)
    left = left_ref[...].astype(jnp.float32)
    right = right_ref[...].astype(jnp.float32)
    before = jnp.where(column == 0, left, pltpu.roll(middle, 1, 1))
    after = jnp.where(column == COLS_IN - 1, right, pltpu.roll(middle, COLS_IN - 1, 1))
    shifted[0] = before.astype(jnp.bfloat16).reshape(height * COLS_IN, C)
    shifted[2] = after.astype(jnp.bfloat16).reshape(height * COLS_IN, C)

    area = ROWS_IN * COLS_IN
    for a in range(2):
        for b in range(2):
            total = None
            for row_offset, row_kernel in tap_table[a]:
                for col_offset, col_kernel in tap_table[b]:
                    window = shifted[col_offset, row_offset * COLS_IN : row_offset * COLS_IN + area]
                    term = dot(window, weight_ref[row_kernel, col_kernel])
                    total = term if total is None else total + term
            for half in range(2):
                part = total[:, half * LANES : (half + 1) * LANES].reshape(ROWS_IN, COLS_IN, LANES)
                joined[half, :, a, pl.ds(b, COLS_IN, stride=2), :] = part
            key_value = dot(total.astype(jnp.bfloat16), kv_weight_ref[...]).astype(jnp.bfloat16)
            at = (2 * a + b) * area
            keys[at : at + area] = key_value[:, :C]
            values[at : at + area] = key_value[:, C:]
    for half in range(2):
        part = joined[half].reshape(2 * ROWS_IN, 2 * COLS_IN, LANES).astype(jnp.bfloat16)
        pixels_ref[:, :, half * LANES : (half + 1) * LANES] = part
    send_pixels = pltpu.make_async_copy(pixels_ref, pixels_hbm, sent)
    send_pixels.start()

    ones = jnp.ones((4 * area, LANES), jnp.bfloat16)
    own_head = iota((1, HEADS, C), 2) // HEAD == iota((1, HEADS, C), 1)
    scores = lax.dot_general(
        wide_queries[...], keys[...], (((1,), (1,)), ((), ())), preferred_element_type=jnp.float32
    )
    highest = jnp.max(scores, axis=1, keepdims=True)
    weights = jnp.exp(scores - highest).astype(jnp.bfloat16)
    summed = dot(weights, values[...]).reshape(PADDED, HEADS, C)
    totals = dot(weights, ones).reshape(PADDED, HEADS, LANES)
    highest = jnp.broadcast_to(highest, (PADDED * HEADS, LANES)).reshape(PADDED, HEADS, LANES)
    here = flags[...] > 0.0
    summed = jnp.sum(jnp.where(own_head, summed, 0.0), axis=1)
    lane = iota((PADDED, HEADS, LANES), 2)
    head = iota((PADDED, HEADS, LANES), 1)
    for half in range(2):
        into = slice(half * PADDED, (half + 1) * PADDED)
        half_sums[into] = jnp.where(here, summed[:, half * LANES : (half + 1) * LANES], 0.0)
        row = lax.rem(iota((PADDED, HEADS, LANES), 0) + half * PADDED, SHARE)
        slot = lane - TILE * row
        own = head - HALF * half
        own = jnp.where((own >= 0) & (own < HALF), own, -TILE * LANES)
        is_highest = slot == own
        placed = jnp.where(is_highest, highest, 0.0) + jnp.where(slot == own + HALF, totals, 0.0)
        absent = jnp.sum(jnp.where(is_highest, masked_low, 0.0), axis=1)
        half_side[into] = jnp.where(here, jnp.sum(placed, axis=1), absent)

    for buffer in (half_sums, half_side):
        buffer[HALVES:] = jnp.zeros((buffer.shape[0] - HALVES, LANES), jnp.float32)
    filled = pl.cdiv(HALVES, SHARE)
    for index in range(filled):
        rows = slice(index * SHARE, (index + 1) * SHARE)
        part_ref[index, :SHARE] = half_sums[rows]
        part_ref[index, SHARE:] = jnp.sum(half_side[rows], axis=0, keepdims=True)
    if filled < part_ref.shape[0]:
        part_ref[filled:] = jnp.zeros((part_ref.shape[0] - filled, TILE, LANES), jnp.float32)
    send_pixels.wait()


def local(x, top, bottom, left, right, weight, kv_weight, wide_queries, flags, shares):
    area = ROWS_IN * COLS_IN
    pixels = jax.ShapeDtypeStruct((2 * ROWS_IN, 2 * COLS_IN, C), jnp.bfloat16)
    vmem = pl.BlockSpec(memory_space=pltpu.VMEM)
    return pl.pallas_call(
        local_kernel,
        out_shape=(pixels, jax.ShapeDtypeStruct((shares, TILE, LANES), jnp.float32)),
        in_specs=[vmem] * 9,
        out_specs=[pl.BlockSpec(memory_space=pltpu.HBM), vmem],
        scratch_shapes=[
            pltpu.VMEM(pixels.shape, pixels.dtype),
            pltpu.VMEM((3, (ROWS_IN + 2) * COLS_IN, C), jnp.bfloat16),
            pltpu.VMEM((2, ROWS_IN, 2, 2 * COLS_IN, LANES), jnp.float32),
            pltpu.VMEM((4 * area, C), jnp.bfloat16),
            pltpu.VMEM((4 * area, C), jnp.bfloat16),
            pltpu.VMEM((HALVES + TILE, LANES), jnp.float32),
            pltpu.VMEM((HALVES + TILE, LANES), jnp.float32),
            pltpu.SemaphoreType.DMA,
        ],
        compiler_params=pltpu.CompilerParams(vmem_limit_bytes=40 << 20),
        cost_estimate=pl.CostEstimate(flops=2_000_000_000, bytes_accessed=4_000_000, transcendentals=800_000),
    )(x, top, bottom, left, right, weight, kv_weight, wide_queries, flags)


def widened(side, first):
    n = side.shape[0]
    lane = iota((n, TILE, LANES), 2)
    own = lane // TILE == iota((n, TILE, LANES), 1)
    rows = jnp.where(own, jnp.broadcast_to(side, (n, TILE, LANES)), 0.0).reshape(n * TILE, LANES)
    spread = iota((LANES, LANES), 0) % TILE - first == iota((LANES, LANES), 1) // HEAD
    return dot_exact(rows, spread.astype(jnp.float32)).reshape(n, TILE, LANES)


def merge(parts):
    n = parts.shape[0]
    side = parts[:, SHARE:, :]
    lane = iota((n, 1, LANES), 2)
    is_highest = (lane % TILE < HALF) & (lane < SHARE * TILE)
    top = jnp.max(side, axis=0, keepdims=True)
    factor = jnp.where(is_highest, jnp.exp(jnp.where(is_highest, side - top, 0.0)), 0.0)
    summed = jnp.sum(parts * widened(factor, 0), axis=0)
    moved = pltpu.roll(factor.reshape(n, LANES), HALF, 1)
    totals = jnp.sum(side.reshape(n, LANES) * moved, axis=0, keepdims=True)
    return summed, jnp.where(is_highest[0], top[0], totals)


def merge_kernel(parts_ref, out_ref):
    summed, side = merge(parts_ref[...])
    row = iota((TILE, LANES), 0)
    merged = jnp.where(row == SHARE, jnp.broadcast_to(side, (TILE, LANES)), summed)
    out_ref[...] = jnp.broadcast_to(merged[None], out_ref.shape)


def attend_kernel(parts_ref, out_ref):
    summed, side = merge(parts_ref[...])
    totals = widened(side[None], HALF)[0]
    attention = jnp.where(iota((TILE, LANES), 0) == SHARE, 0.0, summed / totals)
    out_ref[...] = jnp.broadcast_to(attention[None], out_ref.shape).astype(out_ref.dtype)


def finish_kernel(attention_ref, out_weight_ref, queries_ref, gain_ref, attended_ref, updated_ref, halves):
    shares = attention_ref[...].astype(jnp.float32)
    for index in range(pl.cdiv(HALVES, SHARE)):
        halves[index * SHARE : (index + 1) * SHARE] = shares[index, :SHARE]
    attended = jnp.zeros((PADDED, C), jnp.float32)
    for half in range(2):
        attention = halves[half * PADDED : (half + 1) * PADDED].astype(jnp.bfloat16)
        attended += dot(attention, out_weight_ref[half * LANES : (half + 1) * LANES])
    attended = attended[:QUERIES]
    attended_ref[...] = attended
    residual_sum = queries_ref[...] + attended
    average = jnp.mean(residual_sum, axis=1, keepdims=True)
    centred = residual_sum - average
    deviation = jnp.mean(centred * centred, axis=1, keepdims=True)
    updated_ref[...] = centred * lax.rsqrt(deviation + 1e-05) * gain_ref[...]


def on_device(kernel, out_shape, *operands, scratch=()):
    return pl.pallas_call(
        kernel,
        out_shape=out_shape,
        in_specs=[pl.BlockSpec(memory_space=pltpu.VMEM)] * len(operands),
        out_specs=jax.tree.map(lambda _: pl.BlockSpec(memory_space=pltpu.VMEM), out_shape),
        scratch_shapes=scratch,
        compiler_params=pltpu.CompilerParams(vmem_limit_bytes=32 << 20),
        cost_estimate=pl.CostEstimate(flops=10_000_000, bytes_accessed=500_000, transcendentals=10_000),
    )(*operands)


def neighbours(x, axis, dim):
    peers = lax.axis_size(axis)
    last = lax.slice_in_dim(x, x.shape[dim] - 1, x.shape[dim], axis=dim)
    first = lax.slice_in_dim(x, 0, 1, axis=dim)
    odd = lax.axis_index(axis) % 2 == 1
    swaps = []
    for start, edge in ((0, jnp.where(odd, first, last)), (1, jnp.where(odd, last, first))):
        pairs = [(i, i + 1) for i in range(start, peers - 1, 2)]
        swaps.append(lax.ppermute(edge, axis, pairs + [(j, i) for i, j in pairs]))
    return jnp.where(odd, swaps[0], swaps[1]), jnp.where(odd, swaps[1], swaps[0])


def body(
    features, conv_weight, query_weight, kv_weight, out_weight, queries, norm_gain, active_blocks
):
    top, bottom = neighbours(features, "rows", 0)
    edges = jnp.concatenate(
        [jnp.concatenate([part[:, :1], part[:, -1:]], axis=1) for part in (top, features, bottom)], axis=0
    )
    left, right = neighbours(edges, "cols", 1)
    row_peers, col_peers = lax.axis_size("rows"), lax.axis_size("cols")
    x, weight, kv_weight, wide_queries, flags = prepare(
        features, conv_weight, query_weight, kv_weight, queries, active_blocks
    )
    pixels, part = local(x, top, bottom, left, right, weight, kv_weight, wide_queries, flags, row_peers)
    parts = lax.all_to_all(part, "rows", 0, 0)
    copies = jax.ShapeDtypeStruct((col_peers, TILE, LANES), jnp.float32)
    parts = lax.all_to_all(on_device(merge_kernel, copies, parts), "cols", 0, 0)
    copies = jax.ShapeDtypeStruct((row_peers, TILE, LANES), jnp.bfloat16)
    attention = lax.all_to_all(on_device(attend_kernel, copies, parts), "rows", 0, 0)
    out = jax.ShapeDtypeStruct((QUERIES, C), jnp.float32)
    attended, updated = on_device(
        finish_kernel, (out, out), attention, out_weight, queries, norm_gain.reshape(1, C),
        scratch=[pltpu.VMEM((HALVES + TILE, LANES), jnp.float32)],
    )
    return (pixels, attended, updated)


def solution(mesh):
    placed = (P("rows", "cols", None), P(), P(), P(), P(), P(), P(), P())
    return jax.shard_map(
        body,
        mesh=mesh,
        in_specs=placed,
        out_specs=(P("rows", "cols", None), P(), P()),
        check_vma=False,
    )
```

```python
import functools

import jax
import jax.numpy as jnp
from jax import lax
from jax.experimental import pallas as pl
from jax.experimental.pallas import tpu as pltpu
from jax.sharding import PartitionSpec as P

QUERIES = 100
PADDED = 104
HEADS = 8
HEAD = 32
BLOCK = 32
C = 256
LANES = 128
ROWS_IN = 16
COLS_IN = 16
LIST = 32
HALF = HEADS // 2
SHARE = 7
TILE = 8
HALVES = 2 * PADDED

masked_low = -1e30
tap_table = (((1, 1), (0, 3)), ((1, 2), (2, 0)))


def dot(a, b):
    return jnp.dot(a, b, preferred_element_type=jnp.float32)


def dot_exact(a, b):
    return jnp.dot(a, b, preferred_element_type=jnp.float32, precision=lax.Precision.HIGHEST)


def iota(shape, dim):
    return lax.broadcasted_iota(jnp.int32, shape, dim)


def prepare_kernel(
    after, x_hbm, weight_hbm, query_weight_hbm, kv_weight_hbm, queries_hbm, named_hbm,
    x_ref, weight_ref, kv_weight_ref, wide_queries, flags,
    query_weight_ref, queries_ref, named_ref, spread, arrived
):
    copies = [
        pltpu.make_async_copy(source, target, arrived.at[slot])
        for slot, (source, target) in enumerate((
            (queries_hbm, queries_ref), (query_weight_hbm, query_weight_ref), (named_hbm, named_ref),
            (x_hbm, x_ref), (weight_hbm, weight_ref), (kv_weight_hbm, kv_weight_ref),
        ))
    ]
    for copy in copies:
        copy.start()

    copies[0].wait()
    copies[1].wait()
    projected = dot(queries_ref[...].astype(jnp.bfloat16), query_weight_ref[...]) * HEAD ** (-0.5)
    spread[:QUERIES] = projected
    spread[QUERIES:] = jnp.zeros((PADDED - QUERIES, C), jnp.float32)
    own_head = iota((1, HEADS, C), 2) // HEAD == iota((1, HEADS, C), 1)
    each = jnp.where(own_head, spread[...][:, None, :], 0.0)
    wide_queries[...] = each.reshape(PADDED * HEADS, C).astype(jnp.bfloat16)

    copies[2].wait()
    block_id = lax.axis_index("rows") * lax.axis_size("cols") + lax.axis_index("cols")
    hits = (named_ref[...] == block_id).astype(jnp.bfloat16)
    flags[:QUERIES] = lax.dot_general(
        hits, jnp.ones((hits.shape[0], LANES), jnp.bfloat16), (((0,), (0,)), ((), ())),
        preferred_element_type=jnp.float32,
    )
    flags[QUERIES:] = jnp.zeros((PADDED - QUERIES, LANES), jnp.float32)
    for copy in copies[3:]:
        copy.wait()


def prepare(after, x, weight, query_weight, kv_weight, queries, active_blocks):
    named = active_blocks.T
    operands = [
        pltpu.with_memory_space_constraint(t, pltpu.HBM)
        for t in (x, weight, query_weight, kv_weight, queries, named)
    ]
    vmem = pl.BlockSpec(memory_space=pltpu.VMEM)
    made = (
        x, weight, kv_weight,
        jax.ShapeDtypeStruct((PADDED * HEADS, C), jnp.bfloat16),
        jax.ShapeDtypeStruct((PADDED, LANES), jnp.float32),
    )
    return pl.pallas_call(
        prepare_kernel,
        out_shape=tuple(jax.ShapeDtypeStruct(t.shape, t.dtype) for t in made),
        in_specs=[pl.BlockSpec(memory_space=pl.ANY)] + [pl.BlockSpec(memory_space=pltpu.HBM)] * len(operands),
        out_specs=[vmem] * len(made),
        scratch_shapes=[pltpu.VMEM(t.shape, t.dtype) for t in (query_weight, queries, named)]
        + [pltpu.VMEM((PADDED, C), jnp.float32), pltpu.SemaphoreType.DMA((6,))],
        compiler_params=pltpu.CompilerParams(vmem_limit_bytes=16 << 20),
        cost_estimate=pl.CostEstimate(flops=20_000_000, bytes_accessed=6_000_000, transcendentals=0),
    )(after, *operands)


def middle_kernel(x_ref, left_ref, right_ref, weight_ref, shifted, totals):
    area = ROWS_IN * COLS_IN
    shifted[1] = x_ref[...].reshape(area, C)
    x = x_ref[...].astype(jnp.float32)
    column = iota((ROWS_IN, COLS_IN, C), 1)
    left = left_ref[...].astype(jnp.float32)
    right = right_ref[...].astype(jnp.float32)
    before = jnp.where(column == 0, left, pltpu.roll(x, 1, 1))
    after = jnp.where(column == COLS_IN - 1, right, pltpu.roll(x, COLS_IN - 1, 1))
    shifted[0] = before.astype(jnp.bfloat16).reshape(area, C)
    shifted[2] = after.astype(jnp.bfloat16).reshape(area, C)
    for a in range(2):
        for b in range(2):
            total = None
            for row_offset, row_kernel in tap_table[a]:
                if row_offset == 1:
                    for col_offset, col_kernel in tap_table[b]:
                        term = dot(shifted[col_offset], weight_ref[row_kernel, col_kernel])
                        total = term if total is None else total + term
            totals[2 * a + b] = total


def middle(x, left, right, weight):
    vmem = pl.BlockSpec(memory_space=pltpu.VMEM)
    area = ROWS_IN * COLS_IN
    return pl.pallas_call(
        middle_kernel,
        out_shape=(
            jax.ShapeDtypeStruct((3, area, C), jnp.bfloat16),
            jax.ShapeDtypeStruct((4, area, C), jnp.float32),
        ),
        in_specs=[vmem] * 4,
        out_specs=[vmem] * 2,
        compiler_params=pltpu.CompilerParams(vmem_limit_bytes=16 << 20),
        cost_estimate=pl.CostEstimate(flops=270_000_000, bytes_accessed=3_000_000, transcendentals=0),
    )(x, left, right, weight)


def local_kernel(
    top_ref, bottom_ref, shifted_ref, totals_ref, weight_ref, kv_weight_ref, wide_queries, flags,
    pixels_hbm, part_ref,
    pixels_ref, shifted, joined, keys, values, half_sums, half_side, sent
):
    area = ROWS_IN * COLS_IN
    shifted[:, COLS_IN : COLS_IN + area] = shifted_ref[...]
    for edge_ref, at in ((top_ref, 0), (bottom_ref, COLS_IN + area)):
        edge = edge_ref[0].astype(jnp.float32)
        row, left, right = edge[:COLS_IN], edge[COLS_IN : COLS_IN + 1], edge[COLS_IN + 1 :]
        column = iota((COLS_IN, C), 0)
        into = slice(at, at + COLS_IN)
        shifted[0, into] = jnp.where(column == 0, left, pltpu.roll(row, 1, 0)).astype(jnp.bfloat16)
        shifted[1, into] = row.astype(jnp.bfloat16)
        shifted[2, into] = jnp.where(column == COLS_IN - 1, right, pltpu.roll(row, COLS_IN - 1, 0)).astype(jnp.bfloat16)

    for a in range(2):
        for b in range(2):
            total = totals_ref[2 * a + b]
            for row_offset, row_kernel in tap_table[a]:
                if row_offset != 1:
                    for col_offset, col_kernel in tap_table[b]:
                        window = shifted[col_offset, row_offset * COLS_IN : row_offset * COLS_IN + area]
                        total = total + dot(window, weight_ref[row_kernel, col_kernel])
            for half in range(2):
                part = total[:, half * LANES : (half + 1) * LANES].reshape(ROWS_IN, COLS_IN, LANES)
                joined[half, :, a, pl.ds(b, COLS_IN, stride=2), :] = part
            key_value = dot(total.astype(jnp.bfloat16), kv_weight_ref[...]).astype(jnp.bfloat16)
            at = (2 * a + b) * area
            keys[at : at + area] = key_value[:, :C]
            values[at : at + area] = key_value[:, C:]
    for half in range(2):
        part = joined[half].reshape(2 * ROWS_IN, 2 * COLS_IN, LANES).astype(jnp.bfloat16)
        pixels_ref[:, :, half * LANES : (half + 1) * LANES] = part
    send_pixels = pltpu.make_async_copy(pixels_ref, pixels_hbm, sent)
    send_pixels.start()

    ones = jnp.ones((4 * area, LANES), jnp.bfloat16)
    own_head = iota((1, HEADS, C), 2) // HEAD == iota((1, HEADS, C), 1)
    scores = lax.dot_general(
        wide_queries[...], keys[...], (((1,), (1,)), ((), ())), preferred_element_type=jnp.float32
    )
    highest = jnp.max(scores, axis=1, keepdims=True)
    weights = jnp.exp(scores - highest).astype(jnp.bfloat16)
    summed = dot(weights, values[...]).reshape(PADDED, HEADS, C)
    totals = dot(weights, ones).reshape(PADDED, HEADS, LANES)
    highest = jnp.broadcast_to(highest, (PADDED * HEADS, LANES)).reshape(PADDED, HEADS, LANES)
    here = flags[...] > 0.0
    summed = jnp.sum(jnp.where(own_head, summed, 0.0), axis=1)
    lane = iota((PADDED, HEADS, LANES), 2)
    head = iota((PADDED, HEADS, LANES), 1)
    for half in range(2):
        into = slice(half * PADDED, (half + 1) * PADDED)
        half_sums[into] = jnp.where(here, summed[:, half * LANES : (half + 1) * LANES], 0.0)
        row = lax.rem(iota((PADDED, HEADS, LANES), 0) + half * PADDED, SHARE)
        slot = lane - TILE * row
        own = head - HALF * half
        own = jnp.where((own >= 0) & (own < HALF), own, -TILE * LANES)
        is_highest = slot == own
        placed = jnp.where(is_highest, highest, 0.0) + jnp.where(slot == own + HALF, totals, 0.0)
        absent = jnp.sum(jnp.where(is_highest, masked_low, 0.0), axis=1)
        half_side[into] = jnp.where(here, jnp.sum(placed, axis=1), absent)

    for buffer in (half_sums, half_side):
        buffer[HALVES:] = jnp.zeros((buffer.shape[0] - HALVES, LANES), jnp.float32)
    filled = pl.cdiv(HALVES, SHARE)
    for index in range(filled):
        rows = slice(index * SHARE, (index + 1) * SHARE)
        part_ref[index, :SHARE] = half_sums[rows]
        part_ref[index, SHARE:] = jnp.sum(half_side[rows], axis=0, keepdims=True)
    if filled < part_ref.shape[0]:
        part_ref[filled:] = jnp.zeros((part_ref.shape[0] - filled, TILE, LANES), jnp.float32)
    send_pixels.wait()


def local(top, bottom, shifted, totals, weight, kv_weight, wide_queries, flags, shares):
    area = ROWS_IN * COLS_IN
    pixels = jax.ShapeDtypeStruct((2 * ROWS_IN, 2 * COLS_IN, C), jnp.bfloat16)
    vmem = pl.BlockSpec(memory_space=pltpu.VMEM)
    return pl.pallas_call(
        local_kernel,
        out_shape=(pixels, jax.ShapeDtypeStruct((shares, TILE, LANES), jnp.float32)),
        in_specs=[vmem] * 8,
        out_specs=[pl.BlockSpec(memory_space=pltpu.HBM), vmem],
        scratch_shapes=[
            pltpu.VMEM(pixels.shape, pixels.dtype),
            pltpu.VMEM((3, (ROWS_IN + 2) * COLS_IN, C), jnp.bfloat16),
            pltpu.VMEM((2, ROWS_IN, 2, 2 * COLS_IN, LANES), jnp.float32),
            pltpu.VMEM((4 * area, C), jnp.bfloat16),
            pltpu.VMEM((4 * area, C), jnp.bfloat16),
            pltpu.VMEM((HALVES + TILE, LANES), jnp.float32),
            pltpu.VMEM((HALVES + TILE, LANES), jnp.float32),
            pltpu.SemaphoreType.DMA,
        ],
        compiler_params=pltpu.CompilerParams(vmem_limit_bytes=40 << 20),
        cost_estimate=pl.CostEstimate(flops=2_000_000_000, bytes_accessed=4_000_000, transcendentals=800_000),
    )(top, bottom, shifted, totals, weight, kv_weight, wide_queries, flags)


def widened(side, first):
    n = side.shape[0]
    lane = iota((n, TILE, LANES), 2)
    own = lane // TILE == iota((n, TILE, LANES), 1)
    rows = jnp.where(own, jnp.broadcast_to(side, (n, TILE, LANES)), 0.0).reshape(n * TILE, LANES)
    spread = iota((LANES, LANES), 0) % TILE - first == iota((LANES, LANES), 1) // HEAD
    return dot_exact(rows, spread.astype(jnp.float32)).reshape(n, TILE, LANES)


def merge(parts):
    n = parts.shape[0]
    side = parts[:, SHARE:, :]
    lane = iota((n, 1, LANES), 2)
    is_highest = (lane % TILE < HALF) & (lane < SHARE * TILE)
    top = jnp.max(side, axis=0, keepdims=True)
    factor = jnp.where(is_highest, jnp.exp(jnp.where(is_highest, side - top, 0.0)), 0.0)
    summed = jnp.sum(parts * widened(factor, 0), axis=0)
    moved = pltpu.roll(factor.reshape(n, LANES), HALF, 1)
    totals = jnp.sum(side.reshape(n, LANES) * moved, axis=0, keepdims=True)
    return summed, jnp.where(is_highest[0], top[0], totals)


def merge_kernel(parts_ref, out_ref):
    summed, side = merge(parts_ref[...])
    row = iota((TILE, LANES), 0)
    merged = jnp.where(row == SHARE, jnp.broadcast_to(side, (TILE, LANES)), summed)
    out_ref[...] = jnp.broadcast_to(merged[None], out_ref.shape)


def attend_kernel(parts_ref, out_ref):
    summed, side = merge(parts_ref[...])
    totals = widened(side[None], HALF)[0]
    attention = jnp.where(iota((TILE, LANES), 0) == SHARE, 0.0, summed / totals)
    out_ref[...] = jnp.broadcast_to(attention[None], out_ref.shape).astype(out_ref.dtype)


def finish_kernel(attention_ref, out_weight_ref, queries_ref, gain_ref, attended_ref, updated_ref, halves):
    shares = attention_ref[...].astype(jnp.float32)
    for index in range(pl.cdiv(HALVES, SHARE)):
        halves[index * SHARE : (index + 1) * SHARE] = shares[index, :SHARE]
    attended = jnp.zeros((PADDED, C), jnp.float32)
    for half in range(2):
        attention = halves[half * PADDED : (half + 1) * PADDED].astype(jnp.bfloat16)
        attended += dot(attention, out_weight_ref[half * LANES : (half + 1) * LANES])
    attended = attended[:QUERIES]
    attended_ref[...] = attended
    residual_sum = queries_ref[...] + attended
    average = jnp.mean(residual_sum, axis=1, keepdims=True)
    centred = residual_sum - average
    deviation = jnp.mean(centred * centred, axis=1, keepdims=True)
    updated_ref[...] = centred * lax.rsqrt(deviation + 1e-05) * gain_ref[...]


def on_device(kernel, out_shape, *operands, scratch=()):
    return pl.pallas_call(
        kernel,
        out_shape=out_shape,
        in_specs=[pl.BlockSpec(memory_space=pltpu.VMEM)] * len(operands),
        out_specs=jax.tree.map(lambda _: pl.BlockSpec(memory_space=pltpu.VMEM), out_shape),
        scratch_shapes=scratch,
        compiler_params=pltpu.CompilerParams(vmem_limit_bytes=32 << 20),
        cost_estimate=pl.CostEstimate(flops=10_000_000, bytes_accessed=500_000, transcendentals=10_000),
    )(*operands)


def swaps(first, last, axis):
    peers = lax.axis_size(axis)
    odd = lax.axis_index(axis) % 2 == 1
    swapped = {}
    for start, edge in ((1, jnp.where(odd, last, first)), (0, jnp.where(odd, first, last))):
        pairs = [(i, i + 1) for i in range(start, peers - 1, 2)]
        swapped[start] = lax.ppermute(edge, axis, pairs + [(j, i) for i, j in pairs])
    if axis == 'rows':
        return jnp.where(odd, swapped[0], swapped[1]), jnp.where(odd, swapped[1], swapped[0])
    even = jnp.logical_not(odd)
    return jnp.where(even, swapped[1], swapped[0]), jnp.where(even, swapped[0], swapped[1])


def body(
    features, conv_weight, query_weight, kv_weight, out_weight, queries, norm_gain, active_blocks
):
    left, right = swaps(features[:, :1], features[:, -1:], "cols")
    first, last = [
        jnp.concatenate([part[at : at + 1] for part in (features, left, right)], axis=1) for at in (0, ROWS_IN - 1)
    ]
    top, bottom = swaps(first, last, "rows")
    x, weight, kv_weight, wide_queries, flags = prepare(
        left, features, conv_weight, query_weight, kv_weight, queries, active_blocks
    )
    row_peers, col_peers = lax.axis_size("rows"), lax.axis_size("cols")
    shifted, totals = middle(x, left, right, weight)
    pixels, part = local(top, bottom, shifted, totals, weight, kv_weight, wide_queries, flags, row_peers)
    parts = lax.all_to_all(part, "rows", 0, 0)
    copies = jax.ShapeDtypeStruct((col_peers, TILE, LANES), jnp.float32)
    parts = lax.all_to_all(on_device(merge_kernel, copies, parts), "cols", 0, 0)
    copies = jax.ShapeDtypeStruct((row_peers, TILE, LANES), jnp.bfloat16)
    attention = lax.all_to_all(on_device(attend_kernel, copies, parts), "rows", 0, 0)
    out = jax.ShapeDtypeStruct((QUERIES, C), jnp.float32)
    attended, updated = on_device(
        finish_kernel, (out, out), attention, out_weight, queries, norm_gain.reshape(1, C),
        scratch=[pltpu.VMEM((HALVES + TILE, LANES), jnp.float32)],
    )
    return (pixels, attended, updated)


def solution(mesh):
    placed = (P("rows", "cols", None), P(), P(), P(), P(), P(), P(), P())
    return jax.shard_map(
        body,
        mesh=mesh,
        in_specs=placed,
        out_specs=(P("rows", "cols", None), P(), P()),
        check_vma=False,
    )
```

```python
import functools

import jax
import jax.numpy as jnp
from jax import lax
from jax.experimental import pallas as pl
from jax.experimental.pallas import tpu as pltpu
from jax.sharding import PartitionSpec as P

QUERIES = 100
PADDED = 104
HEADS = 8
HEAD = 32
BLOCK = 32
C = 256
LANES = 128
ROWS_IN = 16
COLS_IN = 16
LIST = 32
HALF = HEADS // 2
SHARE = 7
TILE = 8
HALVES = 2 * PADDED

sizes = (16, 32, 48, PADDED)

masked_low = -1e30
tap_table = (((1, 1), (0, 3)), ((1, 2), (2, 0)))


def dot(a, b):
    return jnp.dot(a, b, preferred_element_type=jnp.float32)


def dot_exact(a, b):
    return jnp.dot(a, b, preferred_element_type=jnp.float32, precision=lax.Precision.HIGHEST)


def iota(shape, dim):
    return lax.broadcasted_iota(jnp.int32, shape, dim)


def prepare_kernel(
    after, x_hbm, weight_hbm, query_weight_hbm, kv_weight_hbm, queries_hbm, named_hbm,
    x_ref, weight_ref, kv_weight_ref, wide_queries, places,
    query_weight_ref, queries_ref, named_ref, spread, flags, arrived
):
    copies = [
        pltpu.make_async_copy(source, target, arrived.at[slot])
        for slot, (source, target) in enumerate((
            (queries_hbm, queries_ref), (query_weight_hbm, query_weight_ref), (named_hbm, named_ref),
            (x_hbm, x_ref), (weight_hbm, weight_ref), (kv_weight_hbm, kv_weight_ref),
        ))
    ]
    for copy in copies:
        copy.start()

    copies[0].wait()
    copies[1].wait()
    projected = dot(queries_ref[...].astype(jnp.bfloat16), query_weight_ref[...]) * HEAD ** (-0.5)
    spread[:QUERIES] = projected
    spread[QUERIES:] = jnp.zeros((PADDED - QUERIES, C), jnp.float32)

    copies[2].wait()
    block_id = lax.axis_index("rows") * lax.axis_size("cols") + lax.axis_index("cols")
    hits = (named_ref[...] == block_id).astype(jnp.bfloat16)
    flags[:QUERIES] = lax.dot_general(
        hits, jnp.ones((hits.shape[0], LANES), jnp.bfloat16), (((0,), (0,)), ((), ())),
        preferred_element_type=jnp.float32,
    )
    flags[QUERIES:] = jnp.zeros((PADDED - QUERIES, LANES), jnp.float32)
    active = flags[...] > 0.0
    earlier = (iota((PADDED, PADDED), 1) < iota((PADDED, PADDED), 0)).astype(jnp.bfloat16)
    rank = dot(earlier, active.astype(jnp.bfloat16)).astype(jnp.int32)
    place = (active & (rank == iota((PADDED, LANES), 1))).astype(jnp.bfloat16)
    places[...] = place.astype(jnp.float32)

    chosen = lax.dot_general(
        place, spread[...].astype(jnp.bfloat16), (((0,), (0,)), ((), ())), preferred_element_type=jnp.float32
    )
    own_head = iota((1, HEADS, C), 2) // HEAD == iota((1, HEADS, C), 1)
    each = jnp.where(own_head, chosen[:PADDED][:, None, :], 0.0)
    wide_queries[...] = each.reshape(PADDED * HEADS, C).astype(jnp.bfloat16)
    for copy in copies[3:]:
        copy.wait()


def prepare(after, x, weight, query_weight, kv_weight, queries, active_blocks):
    named = active_blocks.T
    operands = [
        pltpu.with_memory_space_constraint(t, pltpu.HBM)
        for t in (x, weight, query_weight, kv_weight, queries, named)
    ]
    vmem = pl.BlockSpec(memory_space=pltpu.VMEM)
    made = (
        x, weight, kv_weight,
        jax.ShapeDtypeStruct((PADDED * HEADS, C), jnp.bfloat16),
        jax.ShapeDtypeStruct((PADDED, LANES), jnp.float32),
    )
    return pl.pallas_call(
        prepare_kernel,
        out_shape=tuple(jax.ShapeDtypeStruct(t.shape, t.dtype) for t in made),
        in_specs=[pl.BlockSpec(memory_space=pl.ANY)] + [pl.BlockSpec(memory_space=pltpu.HBM)] * len(operands),
        out_specs=[vmem] * len(made),
        scratch_shapes=[pltpu.VMEM(t.shape, t.dtype) for t in (query_weight, queries, named)]
        + [
            pltpu.VMEM((PADDED, C), jnp.float32),
            pltpu.VMEM((PADDED, LANES), jnp.float32),
            pltpu.SemaphoreType.DMA((6,)),
        ],
        compiler_params=pltpu.CompilerParams(vmem_limit_bytes=16 << 20),
        cost_estimate=pl.CostEstimate(flops=20_000_000, bytes_accessed=6_000_000, transcendentals=0),
    )(after, *operands)


def middle_kernel(x_ref, left_ref, right_ref, weight_ref, shifted, totals):
    area = ROWS_IN * COLS_IN
    shifted[1] = x_ref[...].reshape(area, C)
    x = x_ref[...].astype(jnp.float32)
    column = iota((ROWS_IN, COLS_IN, C), 1)
    left = left_ref[...].astype(jnp.float32)
    right = right_ref[...].astype(jnp.float32)
    before = jnp.where(column == 0, left, pltpu.roll(x, 1, 1))
    after = jnp.where(column == COLS_IN - 1, right, pltpu.roll(x, COLS_IN - 1, 1))
    shifted[0] = before.astype(jnp.bfloat16).reshape(area, C)
    shifted[2] = after.astype(jnp.bfloat16).reshape(area, C)
    for a in range(2):
        for b in range(2):
            total = None
            for row_offset, row_kernel in tap_table[a]:
                if row_offset == 1:
                    for col_offset, col_kernel in tap_table[b]:
                        term = dot(shifted[col_offset], weight_ref[row_kernel, col_kernel])
                        total = term if total is None else total + term
            totals[2 * a + b] = total


def middle(x, left, right, weight):
    vmem = pl.BlockSpec(memory_space=pltpu.VMEM)
    area = ROWS_IN * COLS_IN
    return pl.pallas_call(
        middle_kernel,
        out_shape=(
            jax.ShapeDtypeStruct((3, area, C), jnp.bfloat16),
            jax.ShapeDtypeStruct((4, area, C), jnp.float32),
        ),
        in_specs=[vmem] * 4,
        out_specs=[vmem] * 2,
        compiler_params=pltpu.CompilerParams(vmem_limit_bytes=16 << 20),
        cost_estimate=pl.CostEstimate(flops=270_000_000, bytes_accessed=3_000_000, transcendentals=0),
    )(x, left, right, weight)


def local_kernel(
    top_ref, bottom_ref, shifted_ref, totals_ref, weight_ref, kv_weight_ref, wide_queries, places,
    pixels_hbm, part_ref,
    pixels_ref, shifted, joined, keys, values, chosen, half_sums, half_side, sent
):
    area = ROWS_IN * COLS_IN
    shifted[:, COLS_IN : COLS_IN + area] = shifted_ref[...]
    for edge_ref, at in ((top_ref, 0), (bottom_ref, COLS_IN + area)):
        edge = edge_ref[0].astype(jnp.float32)
        row, left, right = edge[:COLS_IN], edge[COLS_IN : COLS_IN + 1], edge[COLS_IN + 1 :]
        column = iota((COLS_IN, C), 0)
        into = slice(at, at + COLS_IN)
        shifted[0, into] = jnp.where(column == 0, left, pltpu.roll(row, 1, 0)).astype(jnp.bfloat16)
        shifted[1, into] = row.astype(jnp.bfloat16)
        shifted[2, into] = jnp.where(column == COLS_IN - 1, right, pltpu.roll(row, COLS_IN - 1, 0)).astype(jnp.bfloat16)

    for a in range(2):
        for b in range(2):
            total = totals_ref[2 * a + b]
            for row_offset, row_kernel in tap_table[a]:
                if row_offset != 1:
                    for col_offset, col_kernel in tap_table[b]:
                        window = shifted[col_offset, row_offset * COLS_IN : row_offset * COLS_IN + area]
                        total = total + dot(window, weight_ref[row_kernel, col_kernel])
            for half in range(2):
                part = total[:, half * LANES : (half + 1) * LANES].reshape(ROWS_IN, COLS_IN, LANES)
                joined[half, :, a, pl.ds(b, COLS_IN, stride=2), :] = part
            key_value = dot(total.astype(jnp.bfloat16), kv_weight_ref[...]).astype(jnp.bfloat16)
            at = (2 * a + b) * area
            keys[at : at + area] = key_value[:, :C]
            values[at : at + area] = key_value[:, C:]
    for half in range(2):
        part = joined[half].reshape(2 * ROWS_IN, 2 * COLS_IN, LANES).astype(jnp.bfloat16)
        pixels_ref[:, :, half * LANES : (half + 1) * LANES] = part
    send_pixels = pltpu.make_async_copy(pixels_ref, pixels_hbm, sent)
    send_pixels.start()

    number = jnp.sum(places[...])

    def attend(size):
        scores = lax.dot_general(
            wide_queries[: size * HEADS], keys[...], (((1,), (1,)), ((), ())), preferred_element_type=jnp.float32
        )
        highest = jnp.max(scores, axis=1, keepdims=True)
        weights = jnp.exp(scores - highest).astype(jnp.bfloat16)
        summed = dot(weights, values[...]).reshape(size, HEADS, C)
        ones = jnp.ones((4 * area, LANES), jnp.bfloat16)
        totals = dot(weights, ones).reshape(size, HEADS, LANES)
        highest = jnp.broadcast_to(highest, (size * HEADS, LANES)).reshape(size, HEADS, LANES)
        own_head = iota((1, HEADS, C), 2) // HEAD == iota((1, HEADS, C), 1)
        chosen[:size, :C] = jnp.sum(jnp.where(own_head, summed, 0.0), axis=1)
        lane = iota((1, HEADS, LANES), 2) % TILE
        head = iota((1, HEADS, LANES), 1)
        for half in range(2):
            own = head - HALF * half
            own = jnp.where((own >= 0) & (own < HALF), own, -TILE)
            side = jnp.where(lane == own, highest, 0.0) + jnp.where(lane == own + HALF, totals, 0.0)
            chosen[:size, C + half * LANES : C + (half + 1) * LANES] = jnp.sum(side, axis=1)
        chosen[size:] = jnp.zeros((LANES - size, 2 * C), jnp.float32)

    fewer = -1
    for size in sizes:
        pl.when((number > fewer) & (number <= size))(functools.partial(attend, size))
        fewer = size

    place = places[...].astype(jnp.bfloat16)
    rest = chosen[...]
    ordered = jnp.zeros((PADDED, 2 * C), jnp.float32)
    for _ in range(3):
        piece = rest.astype(jnp.bfloat16)
        rest = rest - piece.astype(jnp.float32)
        ordered = ordered + dot(place, piece)
    here = jnp.sum(places[...], axis=1, keepdims=True) > 0.0
    lane = iota((PADDED, LANES), 1)
    for half in range(2):
        into = slice(half * PADDED, (half + 1) * PADDED)
        half_sums[into] = ordered[:, half * LANES : (half + 1) * LANES]
        row = lax.rem(iota((PADDED, LANES), 0) + half * PADDED, SHARE)
        side = ordered[:, C + half * LANES : C + (half + 1) * LANES]
        absent = jnp.where(lane % TILE < HALF, masked_low, 0.0)
        half_side[into] = jnp.where(lane // TILE == row, jnp.where(here, side, absent), 0.0)

    for buffer in (half_sums, half_side):
        buffer[HALVES:] = jnp.zeros((buffer.shape[0] - HALVES, LANES), jnp.float32)
    filled = pl.cdiv(HALVES, SHARE)
    for index in range(filled):
        rows = slice(index * SHARE, (index + 1) * SHARE)
        part_ref[index, :SHARE] = half_sums[rows]
        part_ref[index, SHARE:] = jnp.sum(half_side[rows], axis=0, keepdims=True)
    if filled < part_ref.shape[0]:
        part_ref[filled:] = jnp.zeros((part_ref.shape[0] - filled, TILE, LANES), jnp.float32)
    send_pixels.wait()


def local(top, bottom, shifted, totals, weight, kv_weight, wide_queries, places, shares):
    area = ROWS_IN * COLS_IN
    pixels = jax.ShapeDtypeStruct((2 * ROWS_IN, 2 * COLS_IN, C), jnp.bfloat16)
    vmem = pl.BlockSpec(memory_space=pltpu.VMEM)
    return pl.pallas_call(
        local_kernel,
        out_shape=(pixels, jax.ShapeDtypeStruct((shares, TILE, LANES), jnp.float32)),
        in_specs=[vmem] * 8,
        out_specs=[pl.BlockSpec(memory_space=pltpu.HBM), vmem],
        scratch_shapes=[
            pltpu.VMEM(pixels.shape, pixels.dtype),
            pltpu.VMEM((3, (ROWS_IN + 2) * COLS_IN, C), jnp.bfloat16),
            pltpu.VMEM((2, ROWS_IN, 2, 2 * COLS_IN, LANES), jnp.float32),
            pltpu.VMEM((4 * area, C), jnp.bfloat16),
            pltpu.VMEM((4 * area, C), jnp.bfloat16),
            pltpu.VMEM((LANES, 2 * C), jnp.float32),
            pltpu.VMEM((HALVES + TILE, LANES), jnp.float32),
            pltpu.VMEM((HALVES + TILE, LANES), jnp.float32),
            pltpu.SemaphoreType.DMA,
        ],
        compiler_params=pltpu.CompilerParams(vmem_limit_bytes=40 << 20),
        cost_estimate=pl.CostEstimate(flops=2_000_000_000, bytes_accessed=4_000_000, transcendentals=800_000),
    )(top, bottom, shifted, totals, weight, kv_weight, wide_queries, places)


def widened(side, first):
    n = side.shape[0]
    lane = iota((n, TILE, LANES), 2)
    own = lane // TILE == iota((n, TILE, LANES), 1)
    rows = jnp.where(own, jnp.broadcast_to(side, (n, TILE, LANES)), 0.0).reshape(n * TILE, LANES)
    spread = iota((LANES, LANES), 0) % TILE - first == iota((LANES, LANES), 1) // HEAD
    return dot_exact(rows, spread.astype(jnp.float32)).reshape(n, TILE, LANES)


def merge(parts):
    n = parts.shape[0]
    side = parts[:, SHARE:, :]
    lane = iota((n, 1, LANES), 2)
    is_highest = (lane % TILE < HALF) & (lane < SHARE * TILE)
    top = jnp.max(side, axis=0, keepdims=True)
    factor = jnp.where(is_highest, jnp.exp(jnp.where(is_highest, side - top, 0.0)), 0.0)
    summed = jnp.sum(parts * widened(factor, 0), axis=0)
    moved = pltpu.roll(factor.reshape(n, LANES), HALF, 1)
    totals = jnp.sum(side.reshape(n, LANES) * moved, axis=0, keepdims=True)
    return summed, jnp.where(is_highest[0], top[0], totals)


def merge_kernel(parts_ref, out_ref):
    summed, side = merge(parts_ref[...])
    row = iota((TILE, LANES), 0)
    merged = jnp.where(row == SHARE, jnp.broadcast_to(side, (TILE, LANES)), summed)
    out_ref[...] = jnp.broadcast_to(merged[None], out_ref.shape)


def attend_kernel(parts_ref, out_ref):
    summed, side = merge(parts_ref[...])
    totals = widened(side[None], HALF)[0]
    attention = jnp.where(iota((TILE, LANES), 0) == SHARE, 0.0, summed / totals)
    out_ref[...] = jnp.broadcast_to(attention[None], out_ref.shape).astype(out_ref.dtype)


def finish_kernel(attention_ref, out_weight_ref, queries_ref, gain_ref, attended_ref, updated_ref, halves):
    shares = attention_ref[...].astype(jnp.float32)
    for index in range(pl.cdiv(HALVES, SHARE)):
        halves[index * SHARE : (index + 1) * SHARE] = shares[index, :SHARE]
    attended = jnp.zeros((PADDED, C), jnp.float32)
    for half in range(2):
        attention = halves[half * PADDED : (half + 1) * PADDED].astype(jnp.bfloat16)
        attended += dot(attention, out_weight_ref[half * LANES : (half + 1) * LANES])
    attended = attended[:QUERIES]
    attended_ref[...] = attended
    residual_sum = queries_ref[...] + attended
    average = jnp.mean(residual_sum, axis=1, keepdims=True)
    centred = residual_sum - average
    deviation = jnp.mean(centred * centred, axis=1, keepdims=True)
    updated_ref[...] = centred * lax.rsqrt(deviation + 1e-05) * gain_ref[...]


def on_device(kernel, out_shape, *operands, scratch=()):
    return pl.pallas_call(
        kernel,
        out_shape=out_shape,
        in_specs=[pl.BlockSpec(memory_space=pltpu.VMEM)] * len(operands),
        out_specs=jax.tree.map(lambda _: pl.BlockSpec(memory_space=pltpu.VMEM), out_shape),
        scratch_shapes=scratch,
        compiler_params=pltpu.CompilerParams(vmem_limit_bytes=32 << 20),
        cost_estimate=pl.CostEstimate(flops=10_000_000, bytes_accessed=500_000, transcendentals=10_000),
    )(*operands)


def swaps(first, last, axis):
    peers = lax.axis_size(axis)
    odd = lax.axis_index(axis) % 2 == 1
    swapped = {}
    for start, edge in ((1, jnp.where(odd, last, first)), (0, jnp.where(odd, first, last))):
        pairs = [(i, i + 1) for i in range(start, peers - 1, 2)]
        swapped[start] = lax.ppermute(edge, axis, pairs + [(j, i) for i, j in pairs])
    if axis == 'rows':
        return jnp.where(odd, swapped[0], swapped[1]), jnp.where(odd, swapped[1], swapped[0])
    even = jnp.logical_not(odd)
    return jnp.where(even, swapped[1], swapped[0]), jnp.where(even, swapped[0], swapped[1])


def body(
    features, conv_weight, query_weight, kv_weight, out_weight, queries, norm_gain, active_blocks
):
    left, right = swaps(features[:, :1], features[:, -1:], "cols")
    first, last = [
        jnp.concatenate([part[at : at + 1] for part in (features, left, right)], axis=1) for at in (0, ROWS_IN - 1)
    ]
    top, bottom = swaps(first, last, "rows")
    x, weight, kv_weight, wide_queries, places = prepare(
        left, features, conv_weight, query_weight, kv_weight, queries, active_blocks
    )
    row_peers, col_peers = lax.axis_size("rows"), lax.axis_size("cols")
    shifted, totals = middle(x, left, right, weight)
    pixels, part = local(top, bottom, shifted, totals, weight, kv_weight, wide_queries, places, row_peers)
    parts = lax.all_to_all(part, "rows", 0, 0)
    copies = jax.ShapeDtypeStruct((col_peers, TILE, LANES), jnp.float32)
    parts = lax.all_to_all(on_device(merge_kernel, copies, parts), "cols", 0, 0)
    copies = jax.ShapeDtypeStruct((row_peers, TILE, LANES), jnp.bfloat16)
    attention = lax.all_to_all(on_device(attend_kernel, copies, parts), "rows", 0, 0)
    out = jax.ShapeDtypeStruct((QUERIES, C), jnp.float32)
    attended, updated = on_device(
        finish_kernel, (out, out), attention, out_weight, queries, norm_gain.reshape(1, C),
        scratch=[pltpu.VMEM((HALVES + TILE, LANES), jnp.float32)],
    )
    return (pixels, attended, updated)


def solution(mesh):
    placed = (P("rows", "cols", None), P(), P(), P(), P(), P(), P(), P())
    return jax.shard_map(
        body,
        mesh=mesh,
        in_specs=placed,
        out_specs=(P("rows", "cols", None), P(), P()),
        check_vma=False,
    )
```

```python
import functools

import jax
import jax.numpy as jnp
from jax import lax
from jax.experimental import pallas as pl
from jax.experimental.pallas import tpu as pltpu
from jax.sharding import PartitionSpec as P

QUERIES = 100
PADDED = 104
HEADS = 8
HEAD = 32
BLOCK = 32
C = 256
LANES = 128
ROWS_IN = 16
COLS_IN = 16
LIST = 32
HALF = HEADS // 2
SHARE = 7
TILE = 8
HALVES = 2 * PADDED

sizes = (16, 32, 48, PADDED)

masked_low = -1e30
tap_table = (((1, 1), (0, 3)), ((1, 2), (2, 0)))


def dot(a, b):
    return jnp.dot(a, b, preferred_element_type=jnp.float32)


def pieces(x):
    found = []
    for _ in range(3):
        found.append(x.astype(jnp.bfloat16))
        x = x - found[-1].astype(jnp.float32)
    return found


def dot_exact(a, b):
    total = jnp.zeros((a.shape[0], b.shape[1]), jnp.float32)
    for piece in pieces(a):
        total = total + dot(piece, b.astype(jnp.bfloat16))
    return total


def iota(shape, dim):
    return lax.broadcasted_iota(jnp.int32, shape, dim)


def prepare_kernel(
    after, x_hbm, weight_hbm, query_weight_hbm, kv_weight_hbm, queries_hbm, named_hbm,
    x_ref, weight_ref, kv_weight_ref, wide_queries, places,
    query_weight_ref, queries_ref, named_ref, spread, flags, arrived
):
    copies = [
        pltpu.make_async_copy(source, target, arrived.at[slot])
        for slot, (source, target) in enumerate((
            (queries_hbm, queries_ref), (query_weight_hbm, query_weight_ref), (named_hbm, named_ref),
            (x_hbm, x_ref), (weight_hbm, weight_ref), (kv_weight_hbm, kv_weight_ref),
        ))
    ]
    for copy in copies:
        copy.start()

    copies[0].wait()
    copies[1].wait()
    projected = dot(queries_ref[...].astype(jnp.bfloat16), query_weight_ref[...]) * HEAD ** (-0.5)
    spread[:QUERIES] = projected
    spread[QUERIES:] = jnp.zeros((PADDED - QUERIES, C), jnp.float32)

    copies[2].wait()
    block_id = lax.axis_index("rows") * lax.axis_size("cols") + lax.axis_index("cols")
    hits = (named_ref[...] == block_id).astype(jnp.bfloat16)
    flags[:QUERIES] = lax.dot_general(
        hits, jnp.ones((hits.shape[0], LANES), jnp.bfloat16), (((0,), (0,)), ((), ())),
        preferred_element_type=jnp.float32,
    )
    flags[QUERIES:] = jnp.zeros((PADDED - QUERIES, LANES), jnp.float32)
    active = flags[...] > 0.0
    earlier = (iota((PADDED, PADDED), 1) < iota((PADDED, PADDED), 0)).astype(jnp.bfloat16)
    rank = dot(earlier, active.astype(jnp.bfloat16)).astype(jnp.int32)
    place = (active & (rank == iota((PADDED, LANES), 1))).astype(jnp.bfloat16)
    places[...] = place.astype(jnp.float32)

    chosen = lax.dot_general(
        place, spread[...].astype(jnp.bfloat16), (((0,), (0,)), ((), ())), preferred_element_type=jnp.float32
    )
    own_head = iota((1, HEADS, C), 2) // HEAD == iota((1, HEADS, C), 1)
    each = jnp.where(own_head, chosen[:PADDED][:, None, :], 0.0)
    wide_queries[...] = each.reshape(PADDED * HEADS, C).astype(jnp.bfloat16)
    for copy in copies[3:]:
        copy.wait()


def prepare(after, x, weight, query_weight, kv_weight, queries, active_blocks):
    named = active_blocks.T
    operands = [
        pltpu.with_memory_space_constraint(t, pltpu.HBM)
        for t in (x, weight, query_weight, kv_weight, queries, named)
    ]
    vmem = pl.BlockSpec(memory_space=pltpu.VMEM)
    made = (
        x, weight, kv_weight,
        jax.ShapeDtypeStruct((PADDED * HEADS, C), jnp.bfloat16),
        jax.ShapeDtypeStruct((PADDED, LANES), jnp.float32),
    )
    return pl.pallas_call(
        prepare_kernel,
        out_shape=tuple(jax.ShapeDtypeStruct(t.shape, t.dtype) for t in made),
        in_specs=[pl.BlockSpec(memory_space=pl.ANY)] + [pl.BlockSpec(memory_space=pltpu.HBM)] * len(operands),
        out_specs=[vmem] * len(made),
        scratch_shapes=[pltpu.VMEM(t.shape, t.dtype) for t in (query_weight, queries, named)]
        + [
            pltpu.VMEM((PADDED, C), jnp.float32),
            pltpu.VMEM((PADDED, LANES), jnp.float32),
            pltpu.SemaphoreType.DMA((6,)),
        ],
        compiler_params=pltpu.CompilerParams(vmem_limit_bytes=16 << 20),
        cost_estimate=pl.CostEstimate(flops=20_000_000, bytes_accessed=6_000_000, transcendentals=0),
    )(after, *operands)


def middle_kernel(x_ref, left_ref, right_ref, weight_ref, shifted, totals):
    area = ROWS_IN * COLS_IN
    shifted[1] = x_ref[...].reshape(area, C)
    x = x_ref[...].astype(jnp.float32)
    column = iota((ROWS_IN, COLS_IN, C), 1)
    left = left_ref[...].astype(jnp.float32)
    right = right_ref[...].astype(jnp.float32)
    before = jnp.where(column == 0, left, pltpu.roll(x, 1, 1))
    after = jnp.where(column == COLS_IN - 1, right, pltpu.roll(x, COLS_IN - 1, 1))
    shifted[0] = before.astype(jnp.bfloat16).reshape(area, C)
    shifted[2] = after.astype(jnp.bfloat16).reshape(area, C)
    for a in range(2):
        for b in range(2):
            total = None
            for row_offset, row_kernel in tap_table[a]:
                if row_offset == 1:
                    for col_offset, col_kernel in tap_table[b]:
                        term = dot(shifted[col_offset], weight_ref[row_kernel, col_kernel])
                        total = term if total is None else total + term
            totals[2 * a + b] = total


def middle(x, left, right, weight):
    vmem = pl.BlockSpec(memory_space=pltpu.VMEM)
    area = ROWS_IN * COLS_IN
    return pl.pallas_call(
        middle_kernel,
        out_shape=(
            jax.ShapeDtypeStruct((3, area, C), jnp.bfloat16),
            jax.ShapeDtypeStruct((4, area, C), jnp.float32),
        ),
        in_specs=[vmem] * 4,
        out_specs=[vmem] * 2,
        compiler_params=pltpu.CompilerParams(vmem_limit_bytes=16 << 20),
        cost_estimate=pl.CostEstimate(flops=270_000_000, bytes_accessed=3_000_000, transcendentals=0),
    )(x, left, right, weight)


def local_kernel(
    top_ref, bottom_ref, shifted_ref, totals_ref, weight_ref, kv_weight_ref, wide_queries, places,
    pixels_hbm, part_ref,
    pixels_ref, shifted, joined, keys, values, chosen, half_sums, half_side, sent
):
    area = ROWS_IN * COLS_IN
    shifted[:, COLS_IN : COLS_IN + area] = shifted_ref[...]
    for edge_ref, at in ((top_ref, 0), (bottom_ref, COLS_IN + area)):
        edge = edge_ref[0].astype(jnp.float32)
        row, left, right = edge[:COLS_IN], edge[COLS_IN : COLS_IN + 1], edge[COLS_IN + 1 :]
        column = iota((COLS_IN, C), 0)
        into = slice(at, at + COLS_IN)
        shifted[0, into] = jnp.where(column == 0, left, pltpu.roll(row, 1, 0)).astype(jnp.bfloat16)
        shifted[1, into] = row.astype(jnp.bfloat16)
        shifted[2, into] = jnp.where(column == COLS_IN - 1, right, pltpu.roll(row, COLS_IN - 1, 0)).astype(jnp.bfloat16)

    for a in range(2):
        for b in range(2):
            total = totals_ref[2 * a + b]
            for row_offset, row_kernel in tap_table[a]:
                if row_offset != 1:
                    for col_offset, col_kernel in tap_table[b]:
                        window = shifted[col_offset, row_offset * COLS_IN : row_offset * COLS_IN + area]
                        total = total + dot(window, weight_ref[row_kernel, col_kernel])
            for half in range(2):
                part = total[:, half * LANES : (half + 1) * LANES].reshape(ROWS_IN, COLS_IN, LANES)
                joined[half, :, a, pl.ds(b, COLS_IN, stride=2), :] = part
            key_value = dot(total.astype(jnp.bfloat16), kv_weight_ref[...]).astype(jnp.bfloat16)
            at = (2 * a + b) * area
            keys[at : at + area] = key_value[:, :C]
            values[at : at + area] = key_value[:, C:]
    for half in range(2):
        part = joined[half].reshape(2 * ROWS_IN, 2 * COLS_IN, LANES).astype(jnp.bfloat16)
        pixels_ref[:, :, half * LANES : (half + 1) * LANES] = part
    send_pixels = pltpu.make_async_copy(pixels_ref, pixels_hbm, sent)
    send_pixels.start()

    number = jnp.sum(places[...])

    def attend(size):
        scores = lax.dot_general(
            wide_queries[: size * HEADS], keys[...], (((1,), (1,)), ((), ())), preferred_element_type=jnp.float32
        )
        highest = jnp.max(scores, axis=1, keepdims=True)
        weights = jnp.exp(scores - highest).astype(jnp.bfloat16)
        summed = dot(weights, values[...]).reshape(size, HEADS, C)
        ones = jnp.ones((4 * area, LANES), jnp.bfloat16)
        totals = dot(weights, ones).reshape(size, HEADS, LANES)
        highest = jnp.broadcast_to(highest, (size * HEADS, LANES)).reshape(size, HEADS, LANES)
        own_head = iota((1, HEADS, C), 2) // HEAD == iota((1, HEADS, C), 1)
        chosen[:size, :C] = jnp.sum(jnp.where(own_head, summed, 0.0), axis=1)
        lane = iota((1, HEADS, LANES), 2) % TILE
        head = iota((1, HEADS, LANES), 1)
        for half in range(2):
            own = head - HALF * half
            own = jnp.where((own >= 0) & (own < HALF), own, -TILE)
            side = jnp.where(lane == own, highest, 0.0) + jnp.where(lane == own + HALF, totals, 0.0)
            chosen[:size, C + half * LANES : C + (half + 1) * LANES] = jnp.sum(side, axis=1)
        chosen[size:] = jnp.zeros((LANES - size, 2 * C), jnp.float32)

    fewer = -1
    for size in sizes:
        pl.when((number > fewer) & (number <= size))(functools.partial(attend, size))
        fewer = size

    place = places[...].astype(jnp.bfloat16)
    ordered = jnp.zeros((PADDED, 2 * C), jnp.float32)
    for piece in pieces(chosen[...]):
        ordered = ordered + dot(place, piece)
    here = jnp.sum(places[...], axis=1, keepdims=True) > 0.0
    lane = iota((PADDED, LANES), 1)
    for half in range(2):
        into = slice(half * PADDED, (half + 1) * PADDED)
        half_sums[into] = ordered[:, half * LANES : (half + 1) * LANES]
        row = lax.rem(iota((PADDED, LANES), 0) + half * PADDED, SHARE)
        side = ordered[:, C + half * LANES : C + (half + 1) * LANES]
        absent = jnp.where(lane % TILE < HALF, masked_low, 0.0)
        half_side[into] = jnp.where(lane // TILE == row, jnp.where(here, side, absent), 0.0)

    for buffer in (half_sums, half_side):
        buffer[HALVES:] = jnp.zeros((buffer.shape[0] - HALVES, LANES), jnp.float32)
    filled = pl.cdiv(HALVES, SHARE)
    for index in range(filled):
        rows = slice(index * SHARE, (index + 1) * SHARE)
        part_ref[index, :SHARE] = half_sums[rows]
        part_ref[index, SHARE:] = jnp.sum(half_side[rows], axis=0, keepdims=True)
    if filled < part_ref.shape[0]:
        part_ref[filled:] = jnp.zeros((part_ref.shape[0] - filled, TILE, LANES), jnp.float32)
    send_pixels.wait()


def local(top, bottom, shifted, totals, weight, kv_weight, wide_queries, places, shares):
    area = ROWS_IN * COLS_IN
    pixels = jax.ShapeDtypeStruct((2 * ROWS_IN, 2 * COLS_IN, C), jnp.bfloat16)
    vmem = pl.BlockSpec(memory_space=pltpu.VMEM)
    return pl.pallas_call(
        local_kernel,
        out_shape=(pixels, jax.ShapeDtypeStruct((shares, TILE, LANES), jnp.float32)),
        in_specs=[vmem] * 8,
        out_specs=[pl.BlockSpec(memory_space=pltpu.HBM), vmem],
        scratch_shapes=[
            pltpu.VMEM(pixels.shape, pixels.dtype),
            pltpu.VMEM((3, (ROWS_IN + 2) * COLS_IN, C), jnp.bfloat16),
            pltpu.VMEM((2, ROWS_IN, 2, 2 * COLS_IN, LANES), jnp.float32),
            pltpu.VMEM((4 * area, C), jnp.bfloat16),
            pltpu.VMEM((4 * area, C), jnp.bfloat16),
            pltpu.VMEM((LANES, 2 * C), jnp.float32),
            pltpu.VMEM((HALVES + TILE, LANES), jnp.float32),
            pltpu.VMEM((HALVES + TILE, LANES), jnp.float32),
            pltpu.SemaphoreType.DMA,
        ],
        compiler_params=pltpu.CompilerParams(vmem_limit_bytes=40 << 20),
        cost_estimate=pl.CostEstimate(flops=2_000_000_000, bytes_accessed=4_000_000, transcendentals=800_000),
    )(top, bottom, shifted, totals, weight, kv_weight, wide_queries, places)


def widened(side, first):
    n = side.shape[0]
    lane = iota((n, TILE, LANES), 2)
    own = lane // TILE == iota((n, TILE, LANES), 1)
    rows = jnp.where(own, jnp.broadcast_to(side, (n, TILE, LANES)), 0.0).reshape(n * TILE, LANES)
    spread = iota((LANES, LANES), 0) % TILE - first == iota((LANES, LANES), 1) // HEAD
    return dot_exact(rows, spread.astype(jnp.float32)).reshape(n, TILE, LANES)


def merge(parts):
    n = parts.shape[0]
    side = parts[:, SHARE:, :]
    lane = iota((n, 1, LANES), 2)
    is_highest = (lane % TILE < HALF) & (lane < SHARE * TILE)
    top = jnp.max(side, axis=0, keepdims=True)
    factor = jnp.where(is_highest, jnp.exp(jnp.where(is_highest, side - top, 0.0)), 0.0)
    summed = jnp.sum(parts * widened(factor, 0), axis=0)
    moved = pltpu.roll(factor.reshape(n, LANES), HALF, 1)
    totals = jnp.sum(side.reshape(n, LANES) * moved, axis=0, keepdims=True)
    return summed, jnp.where(is_highest[0], top[0], totals)


def merge_kernel(parts_ref, out_ref):
    summed, side = merge(parts_ref[...])
    row = iota((TILE, LANES), 0)
    merged = jnp.where(row == SHARE, jnp.broadcast_to(side, (TILE, LANES)), summed)
    out_ref[...] = jnp.broadcast_to(merged[None], out_ref.shape)


def attend_kernel(parts_ref, out_ref):
    summed, side = merge(parts_ref[...])
    totals = widened(side[None], HALF)[0]
    attention = jnp.where(iota((TILE, LANES), 0) == SHARE, 0.0, summed / totals)
    out_ref[...] = jnp.broadcast_to(attention[None], out_ref.shape).astype(out_ref.dtype)


def finish_kernel(attention_ref, out_weight_ref, queries_ref, gain_ref, attended_ref, updated_ref, halves):
    shares = attention_ref[...].astype(jnp.float32)
    for index in range(pl.cdiv(HALVES, SHARE)):
        halves[index * SHARE : (index + 1) * SHARE] = shares[index, :SHARE]
    attended = jnp.zeros((PADDED, C), jnp.float32)
    for half in range(2):
        attention = halves[half * PADDED : (half + 1) * PADDED].astype(jnp.bfloat16)
        attended += dot(attention, out_weight_ref[half * LANES : (half + 1) * LANES])
    attended = attended[:QUERIES]
    attended_ref[...] = attended
    residual_sum = queries_ref[...] + attended
    average = jnp.mean(residual_sum, axis=1, keepdims=True)
    centred = residual_sum - average
    deviation = jnp.mean(centred * centred, axis=1, keepdims=True)
    updated_ref[...] = centred * lax.rsqrt(deviation + 1e-05) * gain_ref[...]


def on_device(kernel, out_shape, *operands, scratch=()):
    return pl.pallas_call(
        kernel,
        out_shape=out_shape,
        in_specs=[pl.BlockSpec(memory_space=pltpu.VMEM)] * len(operands),
        out_specs=jax.tree.map(lambda _: pl.BlockSpec(memory_space=pltpu.VMEM), out_shape),
        scratch_shapes=scratch,
        compiler_params=pltpu.CompilerParams(vmem_limit_bytes=32 << 20),
        cost_estimate=pl.CostEstimate(flops=10_000_000, bytes_accessed=500_000, transcendentals=10_000),
    )(*operands)


def swaps(first, last, axis):
    peers = lax.axis_size(axis)
    odd = lax.axis_index(axis) % 2 == 1
    swapped = {}
    for start, edge in ((1, jnp.where(odd, last, first)), (0, jnp.where(odd, first, last))):
        pairs = [(i, i + 1) for i in range(start, peers - 1, 2)]
        swapped[start] = lax.ppermute(edge, axis, pairs + [(j, i) for i, j in pairs])
    if axis == 'rows':
        return jnp.where(odd, swapped[0], swapped[1]), jnp.where(odd, swapped[1], swapped[0])
    even = jnp.logical_not(odd)
    return jnp.where(even, swapped[1], swapped[0]), jnp.where(even, swapped[0], swapped[1])


def body(
    features, conv_weight, query_weight, kv_weight, out_weight, queries, norm_gain, active_blocks
):
    left, right = swaps(features[:, :1], features[:, -1:], "cols")
    first, last = [
        jnp.concatenate([part[at : at + 1] for part in (features, left, right)], axis=1) for at in (0, ROWS_IN - 1)
    ]
    top, bottom = swaps(first, last, "rows")
    x, weight, kv_weight, wide_queries, places = prepare(
        left, features, conv_weight, query_weight, kv_weight, queries, active_blocks
    )
    row_peers, col_peers = lax.axis_size("rows"), lax.axis_size("cols")
    shifted, totals = middle(x, left, right, weight)
    pixels, part = local(top, bottom, shifted, totals, weight, kv_weight, wide_queries, places, row_peers)
    parts = lax.all_to_all(part, "rows", 0, 0)
    copies = jax.ShapeDtypeStruct((col_peers, TILE, LANES), jnp.float32)
    parts = lax.all_to_all(on_device(merge_kernel, copies, parts), "cols", 0, 0)
    copies = jax.ShapeDtypeStruct((row_peers, TILE, LANES), jnp.bfloat16)
    attention = lax.all_to_all(on_device(attend_kernel, copies, parts), "rows", 0, 0)
    out = jax.ShapeDtypeStruct((QUERIES, C), jnp.float32)
    attended, updated = on_device(
        finish_kernel, (out, out), attention, out_weight, queries, norm_gain.reshape(1, C),
        scratch=[pltpu.VMEM((HALVES + TILE, LANES), jnp.float32)],
    )
    return (pixels, attended, updated)


def solution(mesh):
    placed = (P("rows", "cols", None), P(), P(), P(), P(), P(), P(), P())
    return jax.shard_map(
        body,
        mesh=mesh,
        in_specs=placed,
        out_specs=(P("rows", "cols", None), P(), P()),
        check_vma=False,
    )
```

```python
import functools

import jax
import jax.numpy as jnp
from jax import lax
from jax.experimental import pallas as pl
from jax.experimental.pallas import tpu as pltpu
from jax.sharding import PartitionSpec as P

QUERIES = 100
PADDED = 104
HEADS = 8
HEAD = 32
BLOCK = 32
C = 256
LANES = 128
ROWS_IN = 16
COLS_IN = 16
LIST = 32
HALF = HEADS // 2
SHARE = 7
TILE = 8
HALVES = 2 * PADDED

sizes = (16, 32, 48, PADDED)

masked_low = -1e30
tap_table = (((1, 1), (0, 3)), ((1, 2), (2, 0)))


def dot(a, b):
    return jnp.dot(a, b, preferred_element_type=jnp.float32)


def pieces(x):
    found = []
    for _ in range(3):
        found.append(x.astype(jnp.bfloat16))
        x = x - found[-1].astype(jnp.float32)
    return found


def dot_exact(a, b):
    total = jnp.zeros((a.shape[0], b.shape[1]), jnp.float32)
    for piece in pieces(a):
        total = total + dot(piece, b.astype(jnp.bfloat16))
    return total


def iota(shape, dim):
    return lax.broadcasted_iota(jnp.int32, shape, dim)


def prepare_kernel(
    after, x_hbm, weight_hbm, query_weight_hbm, kv_weight_hbm, queries_hbm, named_hbm,
    x_ref, weight_ref, kv_weight_ref, wide_queries, places,
    query_weight_ref, queries_ref, named_ref, spread, flags, arrived
):
    copies = [
        pltpu.make_async_copy(source, target, arrived.at[slot])
        for slot, (source, target) in enumerate((
            (queries_hbm, queries_ref), (query_weight_hbm, query_weight_ref), (named_hbm, named_ref),
            (x_hbm, x_ref), (weight_hbm, weight_ref), (kv_weight_hbm, kv_weight_ref),
        ))
    ]
    for copy in copies:
        copy.start()

    copies[0].wait()
    copies[1].wait()
    projected = dot(queries_ref[...].astype(jnp.bfloat16), query_weight_ref[...]) * HEAD ** (-0.5)
    spread[:QUERIES] = projected
    spread[QUERIES:] = jnp.zeros((PADDED - QUERIES, C), jnp.float32)

    copies[2].wait()
    block_id = lax.axis_index("rows") * lax.axis_size("cols") + lax.axis_index("cols")
    hits = (named_ref[...] == block_id).astype(jnp.bfloat16)
    flags[:QUERIES] = lax.dot_general(
        hits, jnp.ones((hits.shape[0], LANES), jnp.bfloat16), (((0,), (0,)), ((), ())),
        preferred_element_type=jnp.float32,
    )
    flags[QUERIES:] = jnp.zeros((PADDED - QUERIES, LANES), jnp.float32)
    active = flags[...] > 0.0
    earlier = (iota((PADDED, PADDED), 1) < iota((PADDED, PADDED), 0)).astype(jnp.bfloat16)
    rank = dot(earlier, active.astype(jnp.bfloat16)).astype(jnp.int32)
    place = (active & (rank == iota((PADDED, LANES), 1))).astype(jnp.bfloat16)
    places[...] = place.astype(jnp.float32)

    chosen = lax.dot_general(
        place, spread[...].astype(jnp.bfloat16), (((0,), (0,)), ((), ())), preferred_element_type=jnp.float32
    )
    own_head = iota((1, HEADS, C), 2) // HEAD == iota((1, HEADS, C), 1)
    each = jnp.where(own_head, chosen[:PADDED][:, None, :], 0.0)
    wide_queries[...] = each.reshape(PADDED * HEADS, C).astype(jnp.bfloat16)
    for copy in copies[3:]:
        copy.wait()


def prepare(after, x, weight, query_weight, kv_weight, queries, active_blocks):
    named = active_blocks.T
    operands = [
        pltpu.with_memory_space_constraint(t, pltpu.HBM)
        for t in (x, weight, query_weight, kv_weight, queries, named)
    ]
    vmem = pl.BlockSpec(memory_space=pltpu.VMEM)
    made = (
        x, weight, kv_weight,
        jax.ShapeDtypeStruct((PADDED * HEADS, C), jnp.bfloat16),
        jax.ShapeDtypeStruct((PADDED, LANES), jnp.float32),
    )
    return pl.pallas_call(
        prepare_kernel,
        out_shape=tuple(jax.ShapeDtypeStruct(t.shape, t.dtype) for t in made),
        in_specs=[pl.BlockSpec(memory_space=pl.ANY)] + [pl.BlockSpec(memory_space=pltpu.HBM)] * len(operands),
        out_specs=[vmem] * len(made),
        scratch_shapes=[pltpu.VMEM(t.shape, t.dtype) for t in (query_weight, queries, named)]
        + [
            pltpu.VMEM((PADDED, C), jnp.float32),
            pltpu.VMEM((PADDED, LANES), jnp.float32),
            pltpu.SemaphoreType.DMA((6,)),
        ],
        compiler_params=pltpu.CompilerParams(vmem_limit_bytes=16 << 20),
        cost_estimate=pl.CostEstimate(flops=20_000_000, bytes_accessed=6_000_000, transcendentals=0),
    )(after, *operands)


def middle_kernel(x_ref, left_ref, right_ref, weight_ref, shifted, totals):
    area = ROWS_IN * COLS_IN
    shifted[1] = x_ref[...].reshape(area, C)
    x = x_ref[...].astype(jnp.float32)
    column = iota((ROWS_IN, COLS_IN, C), 1)
    left = left_ref[...].astype(jnp.float32)[:, None, :]
    right = right_ref[...].astype(jnp.float32)[:, None, :]
    before = jnp.where(column == 0, left, pltpu.roll(x, 1, 1))
    after = jnp.where(column == COLS_IN - 1, right, pltpu.roll(x, COLS_IN - 1, 1))
    shifted[0] = before.astype(jnp.bfloat16).reshape(area, C)
    shifted[2] = after.astype(jnp.bfloat16).reshape(area, C)
    for a in range(2):
        for b in range(2):
            total = None
            for row_offset, row_kernel in tap_table[a]:
                if row_offset == 1:
                    for col_offset, col_kernel in tap_table[b]:
                        term = dot(shifted[col_offset], weight_ref[row_kernel, col_kernel])
                        total = term if total is None else total + term
            totals[2 * a + b] = total


def middle(x, left, right, weight):
    vmem = pl.BlockSpec(memory_space=pltpu.VMEM)
    area = ROWS_IN * COLS_IN
    return pl.pallas_call(
        middle_kernel,
        out_shape=(
            jax.ShapeDtypeStruct((3, area, C), jnp.bfloat16),
            jax.ShapeDtypeStruct((4, area, C), jnp.float32),
        ),
        in_specs=[vmem] * 4,
        out_specs=[vmem] * 2,
        compiler_params=pltpu.CompilerParams(vmem_limit_bytes=16 << 20),
        cost_estimate=pl.CostEstimate(flops=270_000_000, bytes_accessed=3_000_000, transcendentals=0),
    )(x, left, right, weight)


def local_kernel(
    top_ref, bottom_ref, shifted_ref, totals_ref, weight_ref, kv_weight_ref, wide_queries, places,
    pixels_hbm, part_ref,
    pixels_ref, shifted, joined, keys, values, chosen, half_sums, half_side, sent
):
    area = ROWS_IN * COLS_IN
    shifted[:, COLS_IN : COLS_IN + area] = shifted_ref[...]
    for edge_ref, at in ((top_ref, 0), (bottom_ref, COLS_IN + area)):
        edge = edge_ref[0].astype(jnp.float32)
        row, left, right = edge[:COLS_IN], edge[COLS_IN : COLS_IN + 1], edge[COLS_IN + 1 :]
        column = iota((COLS_IN, C), 0)
        into = slice(at, at + COLS_IN)
        shifted[0, into] = jnp.where(column == 0, left, pltpu.roll(row, 1, 0)).astype(jnp.bfloat16)
        shifted[1, into] = row.astype(jnp.bfloat16)
        shifted[2, into] = jnp.where(column == COLS_IN - 1, right, pltpu.roll(row, COLS_IN - 1, 0)).astype(jnp.bfloat16)

    for a in range(2):
        for b in range(2):
            total = totals_ref[2 * a + b]
            for row_offset, row_kernel in tap_table[a]:
                if row_offset != 1:
                    for col_offset, col_kernel in tap_table[b]:
                        window = shifted[col_offset, row_offset * COLS_IN : row_offset * COLS_IN + area]
                        total = total + dot(window, weight_ref[row_kernel, col_kernel])
            for half in range(2):
                part = total[:, half * LANES : (half + 1) * LANES].reshape(ROWS_IN, COLS_IN, LANES)
                joined[half, :, a, pl.ds(b, COLS_IN, stride=2), :] = part
            key_value = dot(total.astype(jnp.bfloat16), kv_weight_ref[...]).astype(jnp.bfloat16)
            at = (2 * a + b) * area
            keys[at : at + area] = key_value[:, :C]
            values[at : at + area] = key_value[:, C:]
    for half in range(2):
        part = joined[half].reshape(2 * ROWS_IN, 2 * COLS_IN, LANES).astype(jnp.bfloat16)
        pixels_ref[:, :, half * LANES : (half + 1) * LANES] = part
    send_pixels = pltpu.make_async_copy(pixels_ref, pixels_hbm, sent)
    send_pixels.start()

    number = jnp.sum(places[...])

    def attend(size):
        scores = lax.dot_general(
            wide_queries[: size * HEADS], keys[...], (((1,), (1,)), ((), ())), preferred_element_type=jnp.float32
        )
        highest = jnp.max(scores, axis=1, keepdims=True)
        weights = jnp.exp(scores - highest).astype(jnp.bfloat16)
        summed = dot(weights, values[...]).reshape(size, HEADS, C)
        ones = jnp.ones((4 * area, LANES), jnp.bfloat16)
        totals = dot(weights, ones).reshape(size, HEADS, LANES)
        highest = jnp.broadcast_to(highest, (size * HEADS, LANES)).reshape(size, HEADS, LANES)
        own_head = iota((1, HEADS, C), 2) // HEAD == iota((1, HEADS, C), 1)
        chosen[:size, :C] = jnp.sum(jnp.where(own_head, summed, 0.0), axis=1)
        lane = iota((1, HEADS, LANES), 2) % TILE
        head = iota((1, HEADS, LANES), 1)
        for half in range(2):
            own = head - HALF * half
            own = jnp.where((own >= 0) & (own < HALF), own, -TILE)
            side = jnp.where(lane == own, highest, 0.0) + jnp.where(lane == own + HALF, totals, 0.0)
            chosen[:size, C + half * LANES : C + (half + 1) * LANES] = jnp.sum(side, axis=1)
        chosen[size:] = jnp.zeros((LANES - size, 2 * C), jnp.float32)

    fewer = -1
    for size in sizes:
        pl.when((number > fewer) & (number <= size))(functools.partial(attend, size))
        fewer = size

    place = places[...].astype(jnp.bfloat16)
    ordered = jnp.zeros((PADDED, 2 * C), jnp.float32)
    for piece in pieces(chosen[...]):
        ordered = ordered + dot(place, piece)
    here = jnp.sum(places[...], axis=1, keepdims=True) > 0.0
    lane = iota((PADDED, LANES), 1)
    for half in range(2):
        into = slice(half * PADDED, (half + 1) * PADDED)
        half_sums[into] = ordered[:, half * LANES : (half + 1) * LANES]
        row = lax.rem(iota((PADDED, LANES), 0) + half * PADDED, SHARE)
        side = ordered[:, C + half * LANES : C + (half + 1) * LANES]
        absent = jnp.where(lane % TILE < HALF, masked_low, 0.0)
        half_side[into] = jnp.where(lane // TILE == row, jnp.where(here, side, absent), 0.0)

    for buffer in (half_sums, half_side):
        buffer[HALVES:] = jnp.zeros((buffer.shape[0] - HALVES, LANES), jnp.float32)
    filled = pl.cdiv(HALVES, SHARE)
    for index in range(filled):
        rows = slice(index * SHARE, (index + 1) * SHARE)
        part_ref[index, :SHARE] = half_sums[rows]
        part_ref[index, SHARE:] = jnp.sum(half_side[rows], axis=0, keepdims=True)
    if filled < part_ref.shape[0]:
        part_ref[filled:] = jnp.zeros((part_ref.shape[0] - filled, TILE, LANES), jnp.float32)
    send_pixels.wait()


def local(top, bottom, shifted, totals, weight, kv_weight, wide_queries, places, shares):
    area = ROWS_IN * COLS_IN
    pixels = jax.ShapeDtypeStruct((2 * ROWS_IN, 2 * COLS_IN, C), jnp.bfloat16)
    vmem = pl.BlockSpec(memory_space=pltpu.VMEM)
    return pl.pallas_call(
        local_kernel,
        out_shape=(pixels, jax.ShapeDtypeStruct((shares, TILE, LANES), jnp.float32)),
        in_specs=[vmem] * 8,
        out_specs=[pl.BlockSpec(memory_space=pltpu.HBM), vmem],
        scratch_shapes=[
            pltpu.VMEM(pixels.shape, pixels.dtype),
            pltpu.VMEM((3, (ROWS_IN + 2) * COLS_IN, C), jnp.bfloat16),
            pltpu.VMEM((2, ROWS_IN, 2, 2 * COLS_IN, LANES), jnp.float32),
            pltpu.VMEM((4 * area, C), jnp.bfloat16),
            pltpu.VMEM((4 * area, C), jnp.bfloat16),
            pltpu.VMEM((LANES, 2 * C), jnp.float32),
            pltpu.VMEM((HALVES + TILE, LANES), jnp.float32),
            pltpu.VMEM((HALVES + TILE, LANES), jnp.float32),
            pltpu.SemaphoreType.DMA,
        ],
        compiler_params=pltpu.CompilerParams(vmem_limit_bytes=40 << 20),
        cost_estimate=pl.CostEstimate(flops=2_000_000_000, bytes_accessed=4_000_000, transcendentals=800_000),
    )(top, bottom, shifted, totals, weight, kv_weight, wide_queries, places)


def widened(side, first):
    n = side.shape[0]
    lane = iota((n, TILE, LANES), 2)
    own = lane // TILE == iota((n, TILE, LANES), 1)
    rows = jnp.where(own, jnp.broadcast_to(side, (n, TILE, LANES)), 0.0).reshape(n * TILE, LANES)
    spread = iota((LANES, LANES), 0) % TILE - first == iota((LANES, LANES), 1) // HEAD
    return dot_exact(rows, spread.astype(jnp.float32)).reshape(n, TILE, LANES)


def merge(parts):
    n = parts.shape[0]
    side = parts[:, SHARE:, :]
    lane = iota((n, 1, LANES), 2)
    is_highest = (lane % TILE < HALF) & (lane < SHARE * TILE)
    top = jnp.max(side, axis=0, keepdims=True)
    factor = jnp.where(is_highest, jnp.exp(jnp.where(is_highest, side - top, 0.0)), 0.0)
    summed = jnp.sum(parts * widened(factor, 0), axis=0)
    moved = pltpu.roll(factor.reshape(n, LANES), HALF, 1)
    totals = jnp.sum(side.reshape(n, LANES) * moved, axis=0, keepdims=True)
    return summed, jnp.where(is_highest[0], top[0], totals)


def merge_kernel(parts_ref, out_ref):
    summed, side = merge(parts_ref[...])
    row = iota((TILE, LANES), 0)
    merged = jnp.where(row == SHARE, jnp.broadcast_to(side, (TILE, LANES)), summed)
    out_ref[...] = jnp.broadcast_to(merged[None], out_ref.shape)


def attend_kernel(parts_ref, out_ref):
    summed, side = merge(parts_ref[...])
    totals = widened(side[None], HALF)[0]
    attention = jnp.where(iota((TILE, LANES), 0) == SHARE, 0.0, summed / totals)
    out_ref[...] = jnp.broadcast_to(attention[None], out_ref.shape).astype(out_ref.dtype)


def finish_kernel(attention_ref, out_weight_ref, queries_ref, gain_ref, attended_ref, updated_ref, halves):
    shares = attention_ref[...].astype(jnp.float32)
    for index in range(pl.cdiv(HALVES, SHARE)):
        halves[index * SHARE : (index + 1) * SHARE] = shares[index, :SHARE]
    attended = jnp.zeros((PADDED, C), jnp.float32)
    for half in range(2):
        attention = halves[half * PADDED : (half + 1) * PADDED].astype(jnp.bfloat16)
        attended += dot(attention, out_weight_ref[half * LANES : (half + 1) * LANES])
    attended = attended[:QUERIES]
    attended_ref[...] = attended
    residual_sum = queries_ref[...] + attended
    average = jnp.mean(residual_sum, axis=1, keepdims=True)
    centred = residual_sum - average
    deviation = jnp.mean(centred * centred, axis=1, keepdims=True)
    updated_ref[...] = centred * lax.rsqrt(deviation + 1e-05) * gain_ref[...]


def on_device(kernel, out_shape, *operands, scratch=()):
    return pl.pallas_call(
        kernel,
        out_shape=out_shape,
        in_specs=[pl.BlockSpec(memory_space=pltpu.VMEM)] * len(operands),
        out_specs=jax.tree.map(lambda _: pl.BlockSpec(memory_space=pltpu.VMEM), out_shape),
        scratch_shapes=scratch,
        compiler_params=pltpu.CompilerParams(vmem_limit_bytes=32 << 20),
        cost_estimate=pl.CostEstimate(flops=10_000_000, bytes_accessed=500_000, transcendentals=10_000),
    )(*operands)


def swaps(first, last, axis):
    peers = lax.axis_size(axis)
    odd = lax.axis_index(axis) % 2 == 1
    swapped = {}
    for start, edge in ((1, jnp.where(odd, last, first)), (0, jnp.where(odd, first, last))):
        pairs = [(i, i + 1) for i in range(start, peers - 1, 2)]
        swapped[start] = lax.ppermute(edge, axis, pairs + [(j, i) for i, j in pairs])
    if axis == 'rows':
        return jnp.where(odd, swapped[0], swapped[1]), jnp.where(odd, swapped[1], swapped[0])
    even = jnp.logical_not(odd)
    return jnp.where(even, swapped[1], swapped[0]), jnp.where(even, swapped[0], swapped[1])


def body(
    features, conv_weight, query_weight, kv_weight, out_weight, queries, norm_gain, active_blocks
):
    left, right = swaps(features[:, 0], features[:, -1], "cols")
    first, last = [
        jnp.concatenate([features[at], left[at : at + 1], right[at : at + 1]])[None] for at in (0, ROWS_IN - 1)
    ]
    top, bottom = swaps(first, last, "rows")
    x, weight, kv_weight, wide_queries, places = prepare(
        left, features, conv_weight, query_weight, kv_weight, queries, active_blocks
    )
    row_peers, col_peers = lax.axis_size("rows"), lax.axis_size("cols")
    shifted, totals = middle(x, left, right, weight)
    pixels, part = local(top, bottom, shifted, totals, weight, kv_weight, wide_queries, places, row_peers)
    parts = lax.all_to_all(part, "rows", 0, 0)
    copies = jax.ShapeDtypeStruct((col_peers, TILE, LANES), jnp.float32)
    parts = lax.all_to_all(on_device(merge_kernel, copies, parts), "cols", 0, 0)
    copies = jax.ShapeDtypeStruct((row_peers, TILE, LANES), jnp.bfloat16)
    attention = lax.all_to_all(on_device(attend_kernel, copies, parts), "rows", 0, 0)
    out = jax.ShapeDtypeStruct((QUERIES, C), jnp.float32)
    attended, updated = on_device(
        finish_kernel, (out, out), attention, out_weight, queries, norm_gain.reshape(1, C),
        scratch=[pltpu.VMEM((HALVES + TILE, LANES), jnp.float32)],
    )
    return (pixels, attended, updated)


def solution(mesh):
    placed = (P("rows", "cols", None), P(), P(), P(), P(), P(), P(), P())
    return jax.shard_map(
        body,
        mesh=mesh,
        in_specs=placed,
        out_specs=(P("rows", "cols", None), P(), P()),
        check_vma=False,
    )
```

```python
import functools

import jax
import jax.numpy as jnp
from jax import lax
from jax.experimental import pallas as pl
from jax.experimental.pallas import tpu as pltpu
from jax.sharding import PartitionSpec as P

QUERIES = 100
PADDED = 104
HEADS = 8
HEAD = 32
BLOCK = 32
C = 256
LANES = 128
ROWS_IN = 16
COLS_IN = 16
LIST = 32
HALF = HEADS // 2
SHARE = 7
TILE = 8
HALVES = 2 * PADDED

sizes = (8, 16, 24, 32, 48, PADDED)

masked_low = -1e30
tap_table = (((1, 1), (0, 3)), ((1, 2), (2, 0)))


def dot(a, b):
    return jnp.dot(a, b, preferred_element_type=jnp.float32)


def pieces(x):
    found = []
    for _ in range(3):
        found.append(x.astype(jnp.bfloat16))
        x = x - found[-1].astype(jnp.float32)
    return found


def dot_exact(a, b):
    total = jnp.zeros((a.shape[0], b.shape[1]), jnp.float32)
    for piece in pieces(a):
        total = total + dot(piece, b.astype(jnp.bfloat16))
    return total


def iota(shape, dim):
    return lax.broadcasted_iota(jnp.int32, shape, dim)


def prepare_kernel(
    after, x_hbm, weight_hbm, query_weight_hbm, kv_weight_hbm, queries_hbm, named_hbm,
    x_ref, weight_ref, kv_weight_ref, wide_queries, places,
    query_weight_ref, queries_ref, named_ref, spread, flags, arrived
):
    copies = [
        pltpu.make_async_copy(source, target, arrived.at[slot])
        for slot, (source, target) in enumerate((
            (queries_hbm, queries_ref), (query_weight_hbm, query_weight_ref), (named_hbm, named_ref),
            (x_hbm, x_ref), (weight_hbm, weight_ref), (kv_weight_hbm, kv_weight_ref),
        ))
    ]
    for copy in copies:
        copy.start()

    copies[0].wait()
    copies[1].wait()
    projected = dot(queries_ref[...].astype(jnp.bfloat16), query_weight_ref[...]) * HEAD ** (-0.5)
    spread[:QUERIES] = projected
    spread[QUERIES:] = jnp.zeros((PADDED - QUERIES, C), jnp.float32)

    copies[2].wait()
    block_id = lax.axis_index("rows") * lax.axis_size("cols") + lax.axis_index("cols")
    hits = (named_ref[...] == block_id).astype(jnp.bfloat16)
    flags[:QUERIES] = lax.dot_general(
        hits, jnp.ones((hits.shape[0], LANES), jnp.bfloat16), (((0,), (0,)), ((), ())),
        preferred_element_type=jnp.float32,
    )
    flags[QUERIES:] = jnp.zeros((PADDED - QUERIES, LANES), jnp.float32)
    active = flags[...] > 0.0
    earlier = (iota((PADDED, PADDED), 1) < iota((PADDED, PADDED), 0)).astype(jnp.bfloat16)
    rank = dot(earlier, active.astype(jnp.bfloat16)).astype(jnp.int32)
    place = (active & (rank == iota((PADDED, LANES), 1))).astype(jnp.bfloat16)
    places[...] = place.astype(jnp.float32)

    chosen = lax.dot_general(
        place, spread[...].astype(jnp.bfloat16), (((0,), (0,)), ((), ())), preferred_element_type=jnp.float32
    )
    own_head = iota((1, HEADS, C), 2) // HEAD == iota((1, HEADS, C), 1)
    each = jnp.where(own_head, chosen[:PADDED][:, None, :], 0.0)
    wide_queries[...] = each.reshape(PADDED * HEADS, C).astype(jnp.bfloat16)
    for copy in copies[3:]:
        copy.wait()


def prepare(after, x, weight, query_weight, kv_weight, queries, active_blocks):
    named = active_blocks.T
    operands = [
        pltpu.with_memory_space_constraint(t, pltpu.HBM)
        for t in (x, weight, query_weight, kv_weight, queries, named)
    ]
    vmem = pl.BlockSpec(memory_space=pltpu.VMEM)
    made = (
        x, weight, kv_weight,
        jax.ShapeDtypeStruct((PADDED * HEADS, C), jnp.bfloat16),
        jax.ShapeDtypeStruct((PADDED, LANES), jnp.float32),
    )
    return pl.pallas_call(
        prepare_kernel,
        out_shape=tuple(jax.ShapeDtypeStruct(t.shape, t.dtype) for t in made),
        in_specs=[pl.BlockSpec(memory_space=pl.ANY)] + [pl.BlockSpec(memory_space=pltpu.HBM)] * len(operands),
        out_specs=[vmem] * len(made),
        scratch_shapes=[pltpu.VMEM(t.shape, t.dtype) for t in (query_weight, queries, named)]
        + [
            pltpu.VMEM((PADDED, C), jnp.float32),
            pltpu.VMEM((PADDED, LANES), jnp.float32),
            pltpu.SemaphoreType.DMA((6,)),
        ],
        compiler_params=pltpu.CompilerParams(vmem_limit_bytes=16 << 20),
        cost_estimate=pl.CostEstimate(flops=20_000_000, bytes_accessed=6_000_000, transcendentals=0),
    )(after, *operands)


def middle_kernel(x_ref, left_ref, right_ref, weight_ref, shifted, totals):
    area = ROWS_IN * COLS_IN
    shifted[1] = x_ref[...].reshape(area, C)
    x = x_ref[...].astype(jnp.float32)
    column = iota((ROWS_IN, COLS_IN, C), 1)
    left = left_ref[...].astype(jnp.float32)[:, None, :]
    right = right_ref[...].astype(jnp.float32)[:, None, :]
    before = jnp.where(column == 0, left, pltpu.roll(x, 1, 1))
    after = jnp.where(column == COLS_IN - 1, right, pltpu.roll(x, COLS_IN - 1, 1))
    shifted[0] = before.astype(jnp.bfloat16).reshape(area, C)
    shifted[2] = after.astype(jnp.bfloat16).reshape(area, C)
    for a in range(2):
        for b in range(2):
            total = None
            for row_offset, row_kernel in tap_table[a]:
                if row_offset == 1:
                    for col_offset, col_kernel in tap_table[b]:
                        term = dot(shifted[col_offset], weight_ref[row_kernel, col_kernel])
                        total = term if total is None else total + term
            totals[2 * a + b] = total


def middle(x, left, right, weight):
    vmem = pl.BlockSpec(memory_space=pltpu.VMEM)
    area = ROWS_IN * COLS_IN
    return pl.pallas_call(
        middle_kernel,
        out_shape=(
            jax.ShapeDtypeStruct((3, area, C), jnp.bfloat16),
            jax.ShapeDtypeStruct((4, area, C), jnp.float32),
        ),
        in_specs=[vmem] * 4,
        out_specs=[vmem] * 2,
        compiler_params=pltpu.CompilerParams(vmem_limit_bytes=16 << 20),
        cost_estimate=pl.CostEstimate(flops=270_000_000, bytes_accessed=3_000_000, transcendentals=0),
    )(x, left, right, weight)


def local_kernel(
    top_ref, bottom_ref, shifted_ref, totals_ref, weight_ref, kv_weight_ref, wide_queries, places,
    pixels_hbm, part_ref,
    pixels_ref, shifted, joined, keys, values, chosen, half_sums, half_side, sent
):
    area = ROWS_IN * COLS_IN
    shifted[:, COLS_IN : COLS_IN + area] = shifted_ref[...]
    for edge_ref, at in ((top_ref, 0), (bottom_ref, COLS_IN + area)):
        edge = edge_ref[0].astype(jnp.float32)
        row, left, right = edge[:COLS_IN], edge[COLS_IN : COLS_IN + 1], edge[COLS_IN + 1 :]
        column = iota((COLS_IN, C), 0)
        into = slice(at, at + COLS_IN)
        shifted[0, into] = jnp.where(column == 0, left, pltpu.roll(row, 1, 0)).astype(jnp.bfloat16)
        shifted[1, into] = row.astype(jnp.bfloat16)
        shifted[2, into] = jnp.where(column == COLS_IN - 1, right, pltpu.roll(row, COLS_IN - 1, 0)).astype(jnp.bfloat16)

    for a in range(2):
        for b in range(2):
            total = totals_ref[2 * a + b]
            for row_offset, row_kernel in tap_table[a]:
                if row_offset != 1:
                    for col_offset, col_kernel in tap_table[b]:
                        window = shifted[col_offset, row_offset * COLS_IN : row_offset * COLS_IN + area]
                        total = total + dot(window, weight_ref[row_kernel, col_kernel])
            for half in range(2):
                part = total[:, half * LANES : (half + 1) * LANES].reshape(ROWS_IN, COLS_IN, LANES)
                joined[half, :, a, pl.ds(b, COLS_IN, stride=2), :] = part
            key_value = dot(total.astype(jnp.bfloat16), kv_weight_ref[...]).astype(jnp.bfloat16)
            at = (2 * a + b) * area
            keys[at : at + area] = key_value[:, :C]
            values[at : at + area] = key_value[:, C:]
    for half in range(2):
        part = joined[half].reshape(2 * ROWS_IN, 2 * COLS_IN, LANES).astype(jnp.bfloat16)
        pixels_ref[:, :, half * LANES : (half + 1) * LANES] = part
    send_pixels = pltpu.make_async_copy(pixels_ref, pixels_hbm, sent)
    send_pixels.start()

    number = jnp.sum(places[...])

    def attend(size):
        scores = lax.dot_general(
            wide_queries[: size * HEADS], keys[...], (((1,), (1,)), ((), ())), preferred_element_type=jnp.float32
        )
        highest = jnp.max(scores, axis=1, keepdims=True)
        weights = jnp.exp(scores - highest).astype(jnp.bfloat16)
        summed = dot(weights, values[...]).reshape(size, HEADS, C)
        ones = jnp.ones((4 * area, LANES), jnp.bfloat16)
        totals = dot(weights, ones).reshape(size, HEADS, LANES)
        highest = jnp.broadcast_to(highest, (size * HEADS, LANES)).reshape(size, HEADS, LANES)
        own_head = iota((1, HEADS, C), 2) // HEAD == iota((1, HEADS, C), 1)
        chosen[:size, :C] = jnp.sum(jnp.where(own_head, summed, 0.0), axis=1)
        lane = iota((1, HEADS, LANES), 2) % TILE
        head = iota((1, HEADS, LANES), 1)
        for half in range(2):
            own = head - HALF * half
            own = jnp.where((own >= 0) & (own < HALF), own, -TILE)
            side = jnp.where(lane == own, highest, 0.0) + jnp.where(lane == own + HALF, totals, 0.0)
            chosen[:size, C + half * LANES : C + (half + 1) * LANES] = jnp.sum(side, axis=1)
        chosen[size:] = jnp.zeros((LANES - size, 2 * C), jnp.float32)

    fewer = -1
    for size in sizes:
        pl.when((number > fewer) & (number <= size))(functools.partial(attend, size))
        fewer = size

    place = places[...].astype(jnp.bfloat16)
    ordered = jnp.zeros((PADDED, 2 * C), jnp.float32)
    for piece in pieces(chosen[...]):
        ordered = ordered + dot(place, piece)
    here = jnp.sum(places[...], axis=1, keepdims=True) > 0.0
    lane = iota((PADDED, LANES), 1)
    for half in range(2):
        into = slice(half * PADDED, (half + 1) * PADDED)
        half_sums[into] = ordered[:, half * LANES : (half + 1) * LANES]
        row = lax.rem(iota((PADDED, LANES), 0) + half * PADDED, SHARE)
        side = ordered[:, C + half * LANES : C + (half + 1) * LANES]
        absent = jnp.where(lane % TILE < HALF, masked_low, 0.0)
        half_side[into] = jnp.where(lane // TILE == row, jnp.where(here, side, absent), 0.0)

    for buffer in (half_sums, half_side):
        buffer[HALVES:] = jnp.zeros((buffer.shape[0] - HALVES, LANES), jnp.float32)
    filled = pl.cdiv(HALVES, SHARE)
    for index in range(filled):
        rows = slice(index * SHARE, (index + 1) * SHARE)
        part_ref[index, :SHARE] = half_sums[rows]
        part_ref[index, SHARE:] = jnp.sum(half_side[rows], axis=0, keepdims=True)
    if filled < part_ref.shape[0]:
        part_ref[filled:] = jnp.zeros((part_ref.shape[0] - filled, TILE, LANES), jnp.float32)
    send_pixels.wait()


def local(top, bottom, shifted, totals, weight, kv_weight, wide_queries, places, shares):
    area = ROWS_IN * COLS_IN
    pixels = jax.ShapeDtypeStruct((2 * ROWS_IN, 2 * COLS_IN, C), jnp.bfloat16)
    vmem = pl.BlockSpec(memory_space=pltpu.VMEM)
    return pl.pallas_call(
        local_kernel,
        out_shape=(pixels, jax.ShapeDtypeStruct((shares, TILE, LANES), jnp.float32)),
        in_specs=[vmem] * 8,
        out_specs=[pl.BlockSpec(memory_space=pltpu.HBM), vmem],
        scratch_shapes=[
            pltpu.VMEM(pixels.shape, pixels.dtype),
            pltpu.VMEM((3, (ROWS_IN + 2) * COLS_IN, C), jnp.bfloat16),
            pltpu.VMEM((2, ROWS_IN, 2, 2 * COLS_IN, LANES), jnp.float32),
            pltpu.VMEM((4 * area, C), jnp.bfloat16),
            pltpu.VMEM((4 * area, C), jnp.bfloat16),
            pltpu.VMEM((LANES, 2 * C), jnp.float32),
            pltpu.VMEM((HALVES + TILE, LANES), jnp.float32),
            pltpu.VMEM((HALVES + TILE, LANES), jnp.float32),
            pltpu.SemaphoreType.DMA,
        ],
        compiler_params=pltpu.CompilerParams(vmem_limit_bytes=40 << 20),
        cost_estimate=pl.CostEstimate(flops=2_000_000_000, bytes_accessed=4_000_000, transcendentals=800_000),
    )(top, bottom, shifted, totals, weight, kv_weight, wide_queries, places)


def widened(side, first):
    n = side.shape[0]
    lane = iota((n, TILE, LANES), 2)
    own = lane // TILE == iota((n, TILE, LANES), 1)
    rows = jnp.where(own, jnp.broadcast_to(side, (n, TILE, LANES)), 0.0).reshape(n * TILE, LANES)
    spread = iota((LANES, LANES), 0) % TILE - first == iota((LANES, LANES), 1) // HEAD
    return dot_exact(rows, spread.astype(jnp.float32)).reshape(n, TILE, LANES)


def merge(parts):
    n = parts.shape[0]
    side = parts[:, SHARE:, :]
    lane = iota((n, 1, LANES), 2)
    is_highest = (lane % TILE < HALF) & (lane < SHARE * TILE)
    top = jnp.max(side, axis=0, keepdims=True)
    factor = jnp.where(is_highest, jnp.exp(jnp.where(is_highest, side - top, 0.0)), 0.0)
    summed = jnp.sum(parts * widened(factor, 0), axis=0)
    moved = pltpu.roll(factor.reshape(n, LANES), HALF, 1)
    totals = jnp.sum(side.reshape(n, LANES) * moved, axis=0, keepdims=True)
    return summed, jnp.where(is_highest[0], top[0], totals)


def merge_kernel(parts_ref, out_ref):
    summed, side = merge(parts_ref[...])
    row = iota((TILE, LANES), 0)
    merged = jnp.where(row == SHARE, jnp.broadcast_to(side, (TILE, LANES)), summed)
    out_ref[...] = jnp.broadcast_to(merged[None], out_ref.shape)


def attend_kernel(parts_ref, out_ref):
    summed, side = merge(parts_ref[...])
    totals = widened(side[None], HALF)[0]
    attention = jnp.where(iota((TILE, LANES), 0) == SHARE, 0.0, summed / totals)
    out_ref[...] = jnp.broadcast_to(attention[None], out_ref.shape).astype(out_ref.dtype)


def finish_kernel(attention_ref, out_weight_ref, queries_ref, gain_ref, attended_ref, updated_ref, halves):
    shares = attention_ref[...].astype(jnp.float32)
    for index in range(pl.cdiv(HALVES, SHARE)):
        halves[index * SHARE : (index + 1) * SHARE] = shares[index, :SHARE]
    attended = jnp.zeros((PADDED, C), jnp.float32)
    for half in range(2):
        attention = halves[half * PADDED : (half + 1) * PADDED].astype(jnp.bfloat16)
        attended += dot(attention, out_weight_ref[half * LANES : (half + 1) * LANES])
    attended = attended[:QUERIES]
    attended_ref[...] = attended
    residual_sum = queries_ref[...] + attended
    average = jnp.mean(residual_sum, axis=1, keepdims=True)
    centred = residual_sum - average
    deviation = jnp.mean(centred * centred, axis=1, keepdims=True)
    updated_ref[...] = centred * lax.rsqrt(deviation + 1e-05) * gain_ref[...]


def on_device(kernel, out_shape, *operands, scratch=()):
    return pl.pallas_call(
        kernel,
        out_shape=out_shape,
        in_specs=[pl.BlockSpec(memory_space=pltpu.VMEM)] * len(operands),
        out_specs=jax.tree.map(lambda _: pl.BlockSpec(memory_space=pltpu.VMEM), out_shape),
        scratch_shapes=scratch,
        compiler_params=pltpu.CompilerParams(vmem_limit_bytes=32 << 20),
        cost_estimate=pl.CostEstimate(flops=10_000_000, bytes_accessed=500_000, transcendentals=10_000),
    )(*operands)


def swaps(first, last, axis):
    peers = lax.axis_size(axis)
    odd = lax.axis_index(axis) % 2 == 1
    swapped = {}
    for start, edge in ((1, jnp.where(odd, last, first)), (0, jnp.where(odd, first, last))):
        pairs = [(i, i + 1) for i in range(start, peers - 1, 2)]
        swapped[start] = lax.ppermute(edge, axis, pairs + [(j, i) for i, j in pairs])
    if axis == 'rows':
        return jnp.where(odd, swapped[0], swapped[1]), jnp.where(odd, swapped[1], swapped[0])
    even = jnp.logical_not(odd)
    return jnp.where(even, swapped[1], swapped[0]), jnp.where(even, swapped[0], swapped[1])


def body(
    features, conv_weight, query_weight, kv_weight, out_weight, queries, norm_gain, active_blocks
):
    left, right = swaps(features[:, 0], features[:, -1], "cols")
    first, last = [
        jnp.concatenate([features[at], left[at : at + 1], right[at : at + 1]])[None] for at in (0, ROWS_IN - 1)
    ]
    top, bottom = swaps(first, last, "rows")
    x, weight, kv_weight, wide_queries, places = prepare(
        left, features, conv_weight, query_weight, kv_weight, queries, active_blocks
    )
    row_peers, col_peers = lax.axis_size("rows"), lax.axis_size("cols")
    shifted, totals = middle(x, left, right, weight)
    pixels, part = local(top, bottom, shifted, totals, weight, kv_weight, wide_queries, places, row_peers)
    parts = lax.all_to_all(part, "rows", 0, 0)
    copies = jax.ShapeDtypeStruct((col_peers, TILE, LANES), jnp.float32)
    parts = lax.all_to_all(on_device(merge_kernel, copies, parts), "cols", 0, 0)
    copies = jax.ShapeDtypeStruct((row_peers, TILE, LANES), jnp.bfloat16)
    attention = lax.all_to_all(on_device(attend_kernel, copies, parts), "rows", 0, 0)
    out = jax.ShapeDtypeStruct((QUERIES, C), jnp.float32)
    attended, updated = on_device(
        finish_kernel, (out, out), attention, out_weight, queries, norm_gain.reshape(1, C),
        scratch=[pltpu.VMEM((HALVES + TILE, LANES), jnp.float32)],
    )
    return (pixels, attended, updated)


def solution(mesh):
    placed = (P("rows", "cols", None), P(), P(), P(), P(), P(), P(), P())
    return jax.shard_map(
        body,
        mesh=mesh,
        in_specs=placed,
        out_specs=(P("rows", "cols", None), P(), P()),
        check_vma=False,
    )
```
